32 devices in a mesh: grp: 2 (over y), pair: 4 (over z), head: 4 (over x, core).
Axes of the slice: x: 2, y: 2, z: 4, core: 2. Of those that a mesh axis runs over, the one named last changes fastest.
Arguments:
- features: bfloat16 [8, 224, 768], P(('grp', 'pair'), None, 'head'), parts along dimension 0, may hold values from -6 to 6
- pair_list: int32 [8, 2], P('grp'), parts along dimension 0, may hold values from 0 to 3, as said below
- gain_self: float32 [768], replicated, may hold values from 0.1 to 1.9
- gain_memory: float32 [768], replicated, may hold values from 0.1 to 1.9
- gain_cross: float32 [768], replicated, may hold values from 0.1 to 1.9
- gain_mlp: float32 [768], replicated, may hold values from 0.1 to 1.9
- w_self_qkv: bfloat16 [3, 768, 512], P(None, None, 'head'), may hold values from -3 to 3, as said below
- w_self_out: bfloat16 [512, 768], P('head'), may hold values from -0.25 to 0.25
- w_cross_qkv: bfloat16 [3, 768, 512], P(None, None, 'head'), may hold values from -3 to 3, as said below
- w_cross_out: bfloat16 [512, 768], P('head'), may hold values from -1 to 1
- w_up: bfloat16 [768, 3072], P(None, 'head'), may hold values from -0.21875 to 0.21875
- w_down: bfloat16 [3072, 768], P('head'), may hold values from -0.109375 to 0.109375
Outputs:
- summed: float32 [8, 224, 768], P(('grp', 'pair'), None, 'head'), parts along dimension 0
The draws below stay inside these ranges and needn't reach their ends.
There are 2 independent parts, one for each index of `grp`. The reference program is written for one: setup_inputs(seed, part) draws one part's arguments, and reference() takes and returns one part's arrays. A program takes and returns all parts, laid end to end along the dimension named above; an argument that names none is the same for every part. Nothing has to cross between parts.
Inputs may be any that keep to these rules, and one draw needn't show every extreme that they name: `pair_list`: the two images of a pair differ. Column 0 names one image at most 2 times, and some image exactly 2 times. At most 4 pairs name one image in either column, and some image is named by exactly 4 pairs. `w_self_qkv`: Queries, keys and values stacked along the first dimension. `w_cross_qkv`: Queries, keys and values stacked along the first dimension.
All inputs are finite; a program needn't handle non-finite values.
Results may differ from the reference program's by a relative error of at most 0.02.
Values may be sent and summed in bfloat16 or wider, within the bound.
No kernel may reach another device: no remote copies, remote signals or barrier semaphores. Data moves between devices by JAX's collectives and lax.ppermute only.
A program may use at most 64 MiB of HBM per device.

```python
import math
import jax
import jax.numpy as jnp
from jax import lax

D = 768
FF = 3072
HEAD_DIM = 64
TOK = 224
PAIR_CAP = 2
ATT = 512
IMAGES = 4
PAIRS = 4
DEG_CAP = 4
N_HEAD = 4


def align_weights(key, query_scale):
    key_query, key_fresh, key_value = jax.random.split(key, 3)
    queries = jnp.clip(jax.random.normal(key_query, (D, ATT), jnp.float32), -4.0, 4.0) / math.sqrt(D)
    fresh = jnp.clip(jax.random.normal(key_fresh, (D, ATT), jnp.float32), -4.0, 4.0) / math.sqrt(D)
    values_w = jnp.clip(jax.random.normal(key_value, (D, ATT), jnp.float32), -4.0, 4.0) / math.sqrt(D)
    keys_w = jnp.clip(fresh, -3.0, 3.0)
    return jnp.stack([query_scale * queries, keys_w, values_w]).astype(jnp.bfloat16)


def draw_w_self_qkv(key, part):
    key = jax.random.fold_in(key, 5)
    return align_weights(key, 1.0)


def draw_w_cross_qkv(key, part):
    key = jax.random.fold_in(key, 7)
    return align_weights(key, 2.0)


def draw_features(key, part):
    key = jax.random.fold_in(key, 13)
    key_offset, key_noise = jax.random.split(key, 2)
    offset = jnp.clip(jax.random.normal(key_offset, (IMAGES, 1, D), jnp.float32), -3.0, 3.0)
    noise = jax.random.normal(key_noise, (IMAGES, TOK, D), jnp.float32)
    return jnp.clip(1.5 * offset + noise, -6.0, 6.0).astype(jnp.bfloat16)


def draw_pair_list(key, part):
    key = jax.random.fold_in(key, 11)
    key_perm, key_turn, key_shift, key_order = jax.random.split(key, 4)
    others = IMAGES - 1
    ranking = jax.random.permutation(key_perm, IMAGES).astype(jnp.int32)
    turn = jax.random.randint(key_turn, (), 0, others, jnp.int32)
    shift = jax.random.randint(key_shift, (), 1, others, jnp.int32)
    index = jnp.arange(PAIRS, dtype=jnp.int32)
    rest = index - DEG_CAP
    at_hub = index < DEG_CAP
    hub_first = index < PAIR_CAP
    partner_pos = 1 + (index + turn) % others
    first_pos = jnp.where(at_hub, jnp.where(hub_first, 0, partner_pos), 1 + rest % others)
    second_pos = jnp.where(at_hub, jnp.where(hub_first, partner_pos, 0), 1 + (rest + shift) % others)
    listed = jnp.stack([ranking[first_pos], ranking[second_pos]], axis=1)
    order = jax.random.permutation(key_order, PAIRS)
    return listed[order].astype(jnp.int32)


def block_scale(stream_key, extent, shards, low, high):
    def one(dim, parts):
        heights = jax.random.uniform(jax.random.fold_in(jax.random.fold_in(stream_key, 6), dim), (parts,), jnp.float32, low / len(shards), high / len(shards))
        return jnp.repeat(jnp.exp(heights), extent[dim] // parts).reshape((-1,) + (1,) * (len(extent) - dim - 1))

    loudness = one(*shards[0])
    for cut in shards[1:]:
        loudness = loudness * one(*cut)
    return loudness


def scatter_about(rng, extent, scale, most, cuts=(), held_as=jnp.bfloat16):
    level = block_scale(rng, extent, cuts, -0.22, 0.18) if cuts else 1.0
    array = jax.random.normal(rng, extent, jnp.float32) * scale * level
    return jnp.minimum(jnp.maximum(array, -most), most).astype(held_as)


def setup_inputs(seed: int = 0, part: int = 0) -> dict:
    keys = jax.random.split(jax.random.key(seed), 13)
    part_splits = jax.random.split(jax.random.fold_in(keys[12], part), 13)
    features = draw_features(jax.random.fold_in(jax.random.fold_in(keys[12], part), 71), part)
    pair_list = draw_pair_list(jax.random.fold_in(jax.random.fold_in(keys[12], part), 71), part)
    gain_self = jnp.clip(1.0 + 0.18 * jax.random.normal(keys[2], (D,), jnp.float32), 0.1, 1.9)
    gain_memory = jnp.clip(1.0 + 0.18 * jax.random.normal(keys[3], (D,), jnp.float32), 0.1, 1.9)
    gain_cross = jnp.clip(1.0 + 0.18 * jax.random.normal(keys[4], (D,), jnp.float32), 0.1, 1.9)
    gain_mlp = jnp.clip(1.0 + 0.18 * jax.random.normal(keys[5], (D,), jnp.float32), 0.1, 1.9)
    w_self_qkv = draw_w_self_qkv(jax.random.fold_in(keys[12], 71), part)
    w_self_out = scatter_about(keys[7], (ATT, D), ATT ** -0.5, 0.25, ((0, 4),))
    w_cross_qkv = draw_w_cross_qkv(jax.random.fold_in(keys[12], 71), part)
    w_cross_out = scatter_about(keys[9], (ATT, D), (ATT // 16) ** -0.5, 1.0, ((0, 4),))
    w_up = scatter_about(keys[10], (D, FF), D ** -0.5, 0.21875, ((1, 4),))
    w_down = scatter_about(keys[11], (FF, D), FF ** -0.5, 0.109375, ((0, 4),))
    return dict(features=features, pair_list=pair_list, gain_self=gain_self, gain_memory=gain_memory, gain_cross=gain_cross, gain_mlp=gain_mlp, w_self_qkv=w_self_qkv, w_self_out=w_self_out, w_cross_qkv=w_cross_qkv, w_cross_out=w_cross_out, w_up=w_up, w_down=w_down)


def normalize(values_in, scale_gain):
    average = lax.optimization_barrier(jnp.mean(values_in, axis=-1, keepdims=True))
    centred = values_in - average
    variance = lax.optimization_barrier(jnp.mean(centred * centred, axis=-1, keepdims=True))
    return (centred * lax.rsqrt(variance + 1e-06) * scale_gain).astype(jnp.bfloat16)

def split_heads(matrix):
    return matrix.reshape(matrix.shape[:2] + (matrix.shape[2] // HEAD_DIM, HEAD_DIM))

def attend(query_in, key_in, w_qkv):
    queries = jnp.dot(query_in, w_qkv[0], preferred_element_type=jnp.float32).astype(jnp.bfloat16)
    keys_proj = jnp.dot(key_in, w_qkv[1], preferred_element_type=jnp.float32).astype(jnp.bfloat16)
    values_proj = jnp.dot(key_in, w_qkv[2], preferred_element_type=jnp.float32).astype(jnp.bfloat16)
    score_scale = 1.0 / math.sqrt(HEAD_DIM)
    scores = jnp.einsum('vqhd,vkhd->vhqk', split_heads(queries).astype(jnp.float32), split_heads(keys_proj).astype(jnp.float32)) * score_scale
    weights_attn = jax.nn.softmax(scores, axis=-1).astype(jnp.bfloat16)
    context = jnp.einsum('vhqk,vkhd->vqhd', weights_attn.astype(jnp.float32), split_heads(values_proj).astype(jnp.float32)).astype(jnp.bfloat16)
    return context.reshape(queries.shape)

def grouped(values_in, weight):
    col_width = values_in.shape[-1] // N_HEAD
    running = jnp.zeros(values_in.shape[:-1] + (weight.shape[1],), jnp.float32)
    for group_idx in range(N_HEAD):
        lower = group_idx * col_width
        partial_sum = jnp.dot(values_in[..., lower:lower + col_width], weight[lower:lower + col_width], preferred_element_type=jnp.float32)
        running = running + lax.optimization_barrier(partial_sum.astype(jnp.bfloat16)).astype(jnp.float32)
    return running

def decoder_layer(view_feats, memory_feats, gain_self, gain_memory, gain_cross, gain_mlp, w_self_qkv, w_self_out, w_cross_qkv, w_cross_out, w_up, w_down):
    normed_self = normalize(view_feats, gain_self)
    normed_memory = normalize(memory_feats, gain_memory)
    after_self = view_feats + grouped(attend(normed_self, normed_self, w_self_qkv), w_self_out)
    normed_cross = normalize(after_self, gain_cross)
    after_cross = after_self + grouped(attend(normed_cross, normed_memory, w_cross_qkv), w_cross_out)
    normed_mlp = normalize(after_cross, gain_mlp)
    hidden = jax.nn.gelu(jnp.dot(normed_mlp, w_up, preferred_element_type=jnp.float32), approximate=False).astype(jnp.bfloat16)
    return after_cross + grouped(hidden, w_down)

def reference(features, pair_list, gain_self, gain_memory, gain_cross, gain_mlp, w_self_qkv, w_self_out, w_cross_qkv, w_cross_out, w_up, w_down):

    def step_fn(summed, pair_row):
        image_a = pair_row[0]
        image_b = pair_row[1]
        feat_a = lax.dynamic_index_in_dim(features, image_a, 0, keepdims=False)
        feat_b = lax.dynamic_index_in_dim(features, image_b, 0, keepdims=False)
        view_feats = jnp.stack([feat_a, feat_b]).astype(jnp.float32)
        memory_feats = jnp.stack([feat_b, feat_a]).astype(jnp.float32)
        decoded = decoder_layer(view_feats, memory_feats, gain_self, gain_memory, gain_cross, gain_mlp, w_self_qkv, w_self_out, w_cross_qkv, w_cross_out, w_up, w_down)
        summed = summed.at[image_a].add(decoded[0])
        summed = summed.at[image_b].add(decoded[1])
        return (summed, None)
    initial = jnp.zeros(features.shape, jnp.float32)
    summed, unused = lax.scan(step_fn, initial, pair_list)
    return summed
```

```python
import math

import jax
import jax.numpy as jnp
from jax import lax
from jax.experimental import pallas as pl
from jax.experimental.pallas import tpu as pltpu
from jax.sharding import PartitionSpec as P

HEAD_DIM = 64
ROW_GROUPS = 2
DEGREE = 6
SCALE = 1.0 / math.sqrt(HEAD_DIM)
VMEM = pl.BlockSpec(memory_space=pltpu.VMEM)
SMEM = pl.BlockSpec(memory_space=pltpu.SMEM)
BF16 = jnp.bfloat16
F32 = jnp.float32


def mm(a, b):
    return jnp.dot(a, b, preferred_element_type=F32)


def standardize(x):
    centred = x - jnp.mean(x, axis=-1, keepdims=True)
    variance = jnp.mean(centred * centred, axis=-1, keepdims=True)
    return centred * lax.rsqrt(variance + 1e-06)


def head_attention(q, k, v):
    rows, width = q.shape
    heads = width // HEAD_DIM
    lane_head = lax.broadcasted_iota(jnp.int32, (rows, width), 1) // HEAD_DIM
    zero = jnp.zeros_like(q)
    stacked = jnp.concatenate([jnp.where(lane_head == i, q, zero) for i in range(heads)], axis=0)
    scores = lax.dot_general(stacked, k, (((1,), (1,)), ((), ())), preferred_element_type=F32)
    top = jnp.max(scores, axis=-1, keepdims=True)
    weights = jnp.exp((scores - top) * SCALE)
    total = jnp.sum(weights, axis=-1, keepdims=True)
    weights = (weights * (1.0 / total)).astype(BF16)
    mixed = mm(weights, v)
    context = jnp.zeros((rows, width), F32)
    for i in range(heads):
        context = context + jnp.where(lane_head == i, mixed[i * rows : (i + 1) * rows], 0.0)
    return context


def self_kernel(groups, place, *refs):
    blocks = refs[: 2 * groups]
    g_self, g_memory, w_own, w_other, w_kv = refs[2 * groups : 2 * groups + 5]
    x_rows, context, kv, x_full = refs[2 * groups + 5 :]
    group, member = place[0], place[1]
    width = blocks[0].shape[0]
    for step in range(groups):
        source = lax.rem(group - step + groups, groups)
        for other in range(2):
            index = source * 2 + (member if other == 0 else 1 - member)
            x_full[pl.ds(pl.multiple_of(index * width, width), width), :] = blocks[2 * step + other][...]
    x = x_full[...].astype(F32).T
    rows = x.shape[0] // ROW_GROUPS
    normed = standardize(x)
    memory = (normed * g_memory[...]).astype(BF16)
    kv[:, : kv.shape[1] // 2] = mm(memory, w_kv[1]).astype(BF16)
    kv[:, kv.shape[1] // 2 :] = mm(memory, w_kv[2]).astype(BF16)
    own = (normed * g_self[...]).astype(BF16)
    mine = jnp.where(member == 0, own[:rows], own[rows:])
    x_rows[...] = jnp.where(member == 0, x[:rows], x[rows:])
    q = jnp.concatenate([mm(mine, w_own[0]), mm(mine, w_other[0])], axis=1).astype(BF16)
    k = jnp.concatenate([mm(own, w_own[1]), mm(own, w_other[1])], axis=1).astype(BF16)
    v = jnp.concatenate([mm(own, w_own[2]), mm(own, w_other[2])], axis=1).astype(BF16)
    context[...] = head_attention(q, k, v).astype(BF16)


def query_kernel(groups, *refs):
    contexts = refs[:groups]
    w_out = refs[groups : 3 * groups]
    x_rows, gain, wq_own, wq_other, after, queries = refs[3 * groups :]
    total = x_rows[...]
    width = contexts[0].shape[1] // 2
    for step in range(groups):
        total = total + mm(contexts[step][:, :width], w_out[2 * step][...])
        total = total + mm(contexts[step][:, width:], w_out[2 * step + 1][...])
    after[...] = total
    normed = (standardize(total) * gain[...]).astype(BF16)
    queries[...] = jnp.concatenate([mm(normed, wq_own[...]), mm(normed, wq_other[...])], axis=1).astype(BF16)


def cross_kernel(views, queries, *refs):
    own, other, context = refs[:views], refs[views : 2 * views], refs[2 * views]
    q = queries[...]
    width = q.shape[1] // 2
    for view in range(views):
        k = jnp.concatenate([own[view][:, :width], other[view][:, :width]], axis=1)
        v = jnp.concatenate([own[view][:, width:], other[view][:, width:]], axis=1)
        context[view] = head_attention(q, k, v).astype(BF16)


def mlp_kernel(groups, place, counts, *refs):
    contexts = refs[:groups]
    w_out = refs[groups : 3 * groups]
    after, gain, up_own, up_other, down_own, down_other = refs[3 * groups : 3 * groups + 6]
    outs = refs[3 * groups + 6 : 5 * groups + 6]
    kept, partial = refs[5 * groups + 6 :]
    group, member = place[0], place[1]
    views, rows, width = contexts[0].shape
    width = width // 2
    column = after.shape[1] // (2 * groups)
    residual = after[...]
    total = jnp.concatenate([residual] * views, axis=0)
    for step in range(groups):
        held = contexts[step][...].reshape(views * rows, 2 * width)
        total = total + mm(held[:, :width], w_out[2 * step][...])
        total = total + mm(held[:, width:], w_out[2 * step + 1][...])
    share = [counts[view] for view in range(views)]
    keep = jnp.zeros_like(residual)
    for view in range(views):
        keep = keep + share[view] * total[view * rows : (view + 1) * rows]
    kept[...] = keep.T
    normed = (standardize(total) * gain[...]).astype(BF16)
    down = jnp.zeros_like(residual)
    for w_up, w_down in ((up_own, down_own), (up_other, down_other)):
        raw = mm(normed, w_up[...])
        hidden = (0.5 * raw * (1.0 + lax.erf(raw * math.sqrt(0.5)))).astype(BF16).astype(F32)
        added = jnp.zeros((rows, raw.shape[1]), F32)
        for view in range(views):
            added = added + share[view] * hidden[view * rows : (view + 1) * rows]
        down = down + mm(added.astype(BF16), w_down[...])
    partial[...] = down.T
    for step in range(groups):
        target = lax.rem(group + step, groups)
        for other in range(2):
            index = target * 2 + (member if other == 0 else 1 - member)
            here = pl.ds(pl.multiple_of(index * column, column), column)
            piece = partial[here, :]
            if step == 0:
                piece = piece + kept[here, :]
            outs[2 * step + other][...] = piece.astype(outs[2 * step + other].dtype)


def body(
    features,
    pair_list,
    gain_self,
    gain_memory,
    gain_cross,
    gain_mlp,
    w_self_qkv,
    w_self_out,
    w_cross_qkv,
    w_cross_out,
    w_up,
    w_down,
):
    head = lax.axis_size("head")
    groups = head // ROW_GROUPS
    images = lax.axis_size("pair")
    here = lax.axis_index("head")
    image = lax.axis_index("pair")
    group, member = here // ROW_GROUPS, here % ROW_GROUPS
    place = jnp.stack([group, member]).astype(jnp.int32)
    tokens, column = features.shape[1:]
    model = gain_self.shape[0]
    rows = tokens // ROW_GROUPS
    att = w_self_out.shape[0]

    def swap(value):
        return lax.ppermute(value, "head", [(i, i ^ 1) for i in range(head)])

    def turn(value, step, cross=0):
        return lax.ppermute(
            value,
            "head",
            [
                (i, ((i // 2 + step) % groups) * 2 + ((i % 2) ^ cross))
                for i in range(head)
            ],
        )

    def gather_blocks(value):
        blocks = [value, swap(value)]
        for step in range(1, groups):
            arrived = turn(value, step)
            blocks += [arrived, swap(arrived)]
        return blocks

    def call(kernel, out_shape, args, scratch=(), smem=0, flops=0):
        return pl.pallas_call(
            kernel,
            out_shape=out_shape,
            in_specs=[SMEM] * smem + [VMEM] * (len(args) - smem),
            out_specs=jax.tree.map(lambda _: VMEM, out_shape),
            scratch_shapes=list(scratch),
            compiler_params=pltpu.CompilerParams(vmem_limit_bytes=32 * 2**20),
            cost_estimate=pl.CostEstimate(flops=flops, bytes_accessed=2**20, transcendentals=0),
        )(*args)

    shape = jax.ShapeDtypeStruct
    gains = [g.reshape(1, model) for g in (gain_self, gain_memory, gain_cross, gain_mlp)]

    blocks = gather_blocks(features[0].T)
    self_other = swap(w_self_qkv)
    self_out = gather_blocks(w_self_out)
    query_own = w_cross_qkv[0]
    query_other = swap(query_own)
    cross_out = gather_blocks(w_cross_out)
    up_other, down_other = swap(w_up), swap(w_down)

    x_rows, context, kv = call(
        lambda *refs: self_kernel(groups, *refs),
        [
            shape((rows, model), F32),
            shape((rows, 2 * att), BF16),
            shape((tokens, 2 * att), BF16),
        ],
        [place, *blocks, gains[0], gains[1], w_self_qkv, self_other, w_cross_qkv],
        scratch=[pltpu.VMEM((model, tokens), BF16)],
        smem=1,
        flops=10**9,
    )
    contexts = [context] + [turn(context, step) for step in range(1, groups)]

    first, second = pair_list[:, 0], pair_list[:, 1]
    named = (first == image) | (second == image)
    partner = jnp.where(first == image, second, first)
    if images - 1 <= DEGREE:
        views = images - 1
        kv_own = [
            lax.ppermute(kv, "pair", [(i, (i - step) % images) for i in range(images)])
            for step in range(1, images)
        ]
        memories = jnp.stack([(image + step) % images for step in range(1, images)])
        counts = jnp.sum(named[None, :] & (partner[None, :] == memories[:, None]), axis=1)
    else:
        views = min(DEGREE, first.shape[0])
        rank = jnp.cumsum(named.astype(jnp.int32)) - 1
        hit = named[None, :] & (rank[None, :] == jnp.arange(views)[:, None])
        memories = jnp.sum(jnp.where(hit, partner[None, :], 0), axis=1)
        counts = jnp.any(hit, axis=1)
        gathered = lax.all_gather(kv, "pair", axis=0, tiled=False)
        kv_own = [lax.dynamic_index_in_dim(gathered, memories[view], 0, False) for view in range(views)]
    counts = counts.astype(F32)
    kv_other = [swap(value) for value in kv_own]

    after, queries = call(
        lambda *refs: query_kernel(groups, *refs),
        [shape((rows, model), F32), shape((rows, 2 * att), BF16)],
        [*contexts, *self_out, x_rows, gains[2], query_own, query_other],
        flops=10**9,
    )
    context = call(
        lambda *refs: cross_kernel(views, *refs),
        shape((views, rows, 2 * att), BF16),
        [queries, *kv_own, *kv_other],
        flops=10**9,
    )
    contexts = [context] + [turn(context, step) for step in range(1, groups)]
    pieces = call(
        lambda *refs: mlp_kernel(groups, *refs),
        [shape((column, rows), F32)] * 2 + [shape((column, rows), BF16)] * (2 * groups - 2),
        [place, counts, *contexts, *cross_out, after, gains[3], w_up, up_other, w_down, down_other],
        scratch=[pltpu.VMEM((model, rows), F32)] * 2,
        smem=2,
        flops=3 * 10**9,
    )
    mine, theirs = pieces[0], swap(pieces[1])
    for step in range(1, groups):
        mine = mine + turn(pieces[2 * step], step).astype(F32)
        theirs = theirs + turn(pieces[2 * step + 1], step, 1).astype(F32)
    low = jnp.where(member == 0, mine, theirs)
    high = jnp.where(member == 0, theirs, mine)
    return jnp.concatenate([low, high], axis=1).T[None]


def solution(mesh):
    in_specs = (
        P(("grp", "pair"), None, "head"),
        P("grp", None),
        P(),
        P(),
        P(),
        P(),
        P(None, None, "head"),
        P("head", None),
        P(None, None, "head"),
        P("head", None),
        P(None, "head"),
        P("head", None),
    )
    out_specs = P(("grp", "pair"), None, "head")
    return jax.shard_map(body, mesh=mesh, in_specs=in_specs, out_specs=out_specs, check_vma=False)
```

```python
import math

import jax
import jax.numpy as jnp
from jax import lax
from jax.experimental import pallas as pl
from jax.experimental.pallas import tpu as pltpu
from jax.sharding import PartitionSpec as P

HEAD_DIM = 64
ROW_GROUPS = 2
DEGREE = 6
SCALE = 1.0 / math.sqrt(HEAD_DIM)
VMEM = pl.BlockSpec(memory_space=pltpu.VMEM)
SMEM = pl.BlockSpec(memory_space=pltpu.SMEM)
BF16 = jnp.bfloat16
F32 = jnp.float32


def mm(a, b):
    return jnp.dot(a, b, preferred_element_type=F32)


def standardize(x):
    centred = x - jnp.mean(x, axis=-1, keepdims=True)
    variance = jnp.mean(centred * centred, axis=-1, keepdims=True)
    return centred * lax.rsqrt(variance + 1e-06)


def head_attention(q, k, v):
    rows, width = q.shape
    heads = width // HEAD_DIM
    lane_head = lax.broadcasted_iota(jnp.int32, (rows, width), 1) // HEAD_DIM
    zero = jnp.zeros_like(q)
    stacked = jnp.concatenate([jnp.where(lane_head == i, q, zero) for i in range(heads)], axis=0)
    scores = lax.dot_general(stacked, k, (((1,), (1,)), ((), ())), preferred_element_type=F32)
    top = jnp.max(scores, axis=-1, keepdims=True)
    weights = jnp.exp((scores - top) * SCALE)
    total = jnp.sum(weights, axis=-1, keepdims=True)
    weights = (weights * (1.0 / total)).astype(BF16)
    mixed = mm(weights, v)
    context = jnp.zeros((rows, width), F32)
    for i in range(heads):
        context = context + jnp.where(lane_head == i, mixed[i * rows : (i + 1) * rows], 0.0)
    return context


def position():
    here = lax.axis_index("head")
    return here // ROW_GROUPS, lax.rem(here, ROW_GROUPS)


def mark_kernel(block, out):
    out[...] = block[:8, :128].astype(F32)


def self_kernel(groups, *refs):
    blocks = refs[: 2 * groups]
    g_self, g_memory, w_cross, w_own, w_other, out_own, out_other = refs[2 * groups : 2 * groups + 7]
    x_rows, partial, kv, x_full = refs[-4:]
    group, member = position()
    width = blocks[0].shape[0]
    for index in range(2 * groups):
        source = lax.rem(group - index // 2 + groups, groups) * 2
        source = source + (member if index % 2 == 0 else 1 - member)
        x_full[pl.ds(pl.multiple_of(source * width, width), width), :] = blocks[index][...]
    x = x_full[...].astype(F32).T
    rows = x.shape[0] // ROW_GROUPS
    x_rows[...] = jnp.where(member == 0, x[:rows], x[rows:])
    normed = standardize(x)
    memory = (normed * g_memory[...].reshape(1, -1)).astype(BF16)
    kv[:, : kv.shape[1] // 2] = mm(memory, w_cross[1]).astype(BF16)
    kv[:, kv.shape[1] // 2 :] = mm(memory, w_cross[2]).astype(BF16)
    own = (normed * g_self[...].reshape(1, -1)).astype(BF16)
    mine = jnp.where(member == 0, own[:rows], own[rows:])
    q = jnp.concatenate([mm(mine, w_own[0]), mm(mine, w_other[0])], axis=1).astype(BF16)
    k = jnp.concatenate([mm(own, w_own[1]), mm(own, w_other[1])], axis=1).astype(BF16)
    v = jnp.concatenate([mm(own, w_own[2]), mm(own, w_other[2])], axis=1).astype(BF16)
    context = head_attention(q, k, v).astype(BF16)
    width = context.shape[1] // 2
    total = mm(context[:, :width], out_own[...]) + mm(context[:, width:], out_other[...])
    partial[...] = total.astype(BF16)


def query_kernel(x_rows, gain, w_own, w_other, *refs):
    after, kept, given = refs[-3:]
    total = x_rows[...]
    for partial in refs[:-3]:
        total = total + partial[...].astype(F32)
    after[...] = total
    normed = (standardize(total) * gain[...].reshape(1, -1)).astype(BF16)
    kept[...] = mm(normed, w_own[0]).astype(BF16)
    given[...] = mm(normed, w_other[0]).astype(BF16)


def hand_on(passed, handed, sems):
    copies = [pltpu.make_async_copy(passed[i], handed[i], sems.at[i]) for i in range(len(passed))]
    for copy in copies:
        copy.start()
    return copies


def cross_kernel(count, q_own, q_other, *refs):
    passed, refs = refs[:count], refs[count:]
    memories, kept, given = refs[: -3 - count], refs[-3 - count], refs[-2 - count]
    copies = hand_on(passed, refs[len(refs) - 1 - count : -1], refs[-1])
    rows, width = q_own.shape
    q = jnp.concatenate([q_own[...], q_other[...]], axis=0)
    for view, memory in enumerate(memories):
        context = head_attention(q, memory[:, :width], memory[:, width:]).astype(BF16)
        kept[view] = context[:rows]
        given[view] = context[rows:]
    for copy in copies:
        copy.wait()


def other_image(image, step, images):
    return image ^ step if images & (images - 1) == 0 else (image + step) % images


def view_counts(images, pairs):
    image = lax.axis_index("pair")
    counts = []
    for step in range(1, images):
        memory = other_image(image, step, images)
        count = jnp.int32(0)
        for pair in range(pairs.shape[1]):
            first, second = pairs[0, pair], pairs[1, pair]
            named = ((first == image) & (second == memory)) | ((first == memory) & (second == image))
            count = count + jnp.where(named, 1, 0)
        counts.append(count.astype(F32))
    return counts


def mlp_kernel(groups, images, listed, *refs):
    contexts, refs = refs[: 2 * groups], refs[2 * groups :]
    views = contexts[0].shape[0]
    w_out = refs[: 2 * groups]
    after, gain, up_own, up_other, down_own, down_other = refs[2 * groups : 2 * groups + 6]
    outs = refs[2 * groups + 6 : 4 * groups + 6]
    kept, partial = refs[4 * groups + 6 :]
    group, member = position()
    rows = after.shape[0]
    column = after.shape[1] // (2 * groups)
    residual = after[...]
    total = jnp.concatenate([residual] * views, axis=0)
    for source in range(2 * groups):
        held = contexts[source][...].reshape(views * rows, -1)
        total = total + mm(held, w_out[source][...])
    if images:
        share = view_counts(images, listed)
    else:
        share = [listed[view].astype(F32) for view in range(views)]
    keep = jnp.zeros_like(residual)
    for view in range(views):
        keep = keep + share[view] * total[view * rows : (view + 1) * rows]
    kept[...] = keep.T
    normed = (standardize(total) * gain[...].reshape(1, -1)).astype(BF16)
    down = jnp.zeros_like(residual)
    for w_up, w_down in ((up_own, down_own), (up_other, down_other)):
        raw = mm(normed, w_up[...])
        hidden = (0.5 * raw * (1.0 + lax.erf(raw * math.sqrt(0.5)))).astype(BF16).astype(F32)
        added = jnp.zeros((rows, raw.shape[1]), F32)
        for view in range(views):
            added = added + share[view] * hidden[view * rows : (view + 1) * rows]
        down = down + mm(added.astype(BF16), w_down[...])
    partial[...] = down.T
    for step in range(groups):
        target = lax.rem(group + step, groups)
        for other in range(2):
            index = target * 2 + (member if other == 0 else 1 - member)
            here = pl.ds(pl.multiple_of(index * column, column), column)
            piece = partial[here, :]
            if step == 0:
                piece = piece + kept[here, :]
            outs[2 * step + other][...] = piece.astype(outs[2 * step + other].dtype)


def sum_kernel(groups, *refs):
    member = position()[1]
    out = refs[2 * groups]
    rows = refs[0].shape[1]
    mine, theirs = refs[0][...], refs[1][...]
    for step in range(1, groups):
        mine = mine + refs[2 * step][...].astype(F32)
        theirs = theirs + refs[2 * step + 1][...].astype(F32)
    out[:, :rows] = jnp.where(member == 0, mine, theirs)
    out[:, rows:] = jnp.where(member == 0, theirs, mine)


def body(
    features,
    pair_list,
    gain_self,
    gain_memory,
    gain_cross,
    gain_mlp,
    w_self_qkv,
    w_self_out,
    w_cross_qkv,
    w_cross_out,
    w_up,
    w_down,
):
    head = lax.axis_size("head")
    groups = head // ROW_GROUPS
    images = lax.axis_size("pair")
    tokens, column = features.shape[1:]
    model = gain_self.shape[0]
    rows = tokens // ROW_GROUPS
    att = w_self_out.shape[0]

    def swap(value):
        return lax.ppermute(value, "head", [(i, i ^ 1) for i in range(head)])

    def turn(value, step, cross=0):
        return lax.ppermute(
            value,
            "head",
            [
                (i, ((i // 2 + step) % groups) * 2 + ((i % 2) ^ cross))
                for i in range(head)
            ],
        )

    def call(kernel, out_shape, args, scratch=(), smem=0, flops=0, moved=0):
        return pl.pallas_call(
            kernel,
            out_shape=out_shape,
            in_specs=[SMEM] * smem + [VMEM] * (len(args) - smem),
            out_specs=jax.tree.map(lambda _: VMEM, out_shape),
            scratch_shapes=list(scratch),
            compiler_params=pltpu.CompilerParams(vmem_limit_bytes=16 * 2**20),
            cost_estimate=pl.CostEstimate(flops=flops, bytes_accessed=moved, transcendentals=0),
        )(*args)

    def exchange(kept, given):
        blocks = [kept, swap(given)]
        for step in range(1, groups):
            blocks += [turn(kept, step), turn(given, step, 1)]
        return blocks

    shape = jax.ShapeDtypeStruct
    features = features[0].T
    blocks = [features, swap(features)]
    for step in range(1, groups):
        arrived = turn(features, step)
        blocks += [arrived, swap(arrived)]
    turned = [turn(w_cross_out, step) for step in range(1, groups)]
    self_other, self_out_other, cross_other = swap(w_self_qkv), swap(w_self_out), swap(w_cross_qkv)
    up_other, down_other, cross_out_other = swap(w_up), swap(w_down), swap(w_cross_out)

    mark = call(mark_kernel, shape((8, 128), F32), [blocks[1]], flops=3 * 10**9)
    x_rows, partial, kv = call(
        lambda *refs: self_kernel(groups, *refs),
        [shape((rows, model), F32), shape((rows, model), BF16), shape((tokens, 2 * att), BF16)],
        [
            *blocks,
            gain_self,
            gain_memory,
            w_cross_qkv,
            w_self_qkv,
            self_other,
            w_self_out,
            self_out_other,
            mark,
            cross_other,
            up_other,
            down_other,
        ],
        scratch=[pltpu.VMEM((model, tokens), BF16)],
        flops=10**8,
    )

    static = images - 1 <= DEGREE
    if static:
        views = images - 1
        listed = pair_list.T
        kv_own = [
            lax.ppermute(kv, "pair", [(other_image(i, step, images), i) for i in range(images)])
            for step in range(1, images)
        ]
    else:
        views = min(DEGREE, pair_list.shape[0])
        image = lax.axis_index("pair")
        first, second = pair_list[:, 0], pair_list[:, 1]
        named = (first == image) | (second == image)
        partner = jnp.where(first == image, second, first)
        rank = jnp.cumsum(named.astype(jnp.int32)) - 1
        hit = named[None, :] & (rank[None, :] == jnp.arange(views)[:, None])
        memories = jnp.sum(jnp.where(hit, partner[None, :], 0), axis=1)
        listed = jnp.any(hit, axis=1).astype(jnp.int32)
        gathered = lax.all_gather(kv, "pair", axis=0, tiled=False)
        kv_own = [lax.dynamic_index_in_dim(gathered, memories[view], 0, False) for view in range(views)]
    partials = [partial] + [turn(partial, step) for step in range(1, groups)]
    after, q_own, q_given = call(
        query_kernel,
        [shape((rows, model), F32)] + [shape((rows, att), BF16)] * 2,
        [x_rows, gain_cross, w_cross_qkv, cross_other, *partials],
        flops=10**8,
    )
    kept, given, *handed = call(
        lambda *refs: cross_kernel(groups - 1, *refs),
        [shape((views, rows, att), BF16)] * 2 + [shape(value.shape, BF16) for value in turned],
        [q_own, swap(q_given), *turned, *kv_own],
        scratch=[pltpu.SemaphoreType.DMA((max(groups - 1, 1),))],
        flops=10**8,
    )
    contexts = exchange(kept, given)
    cross_out = [w_cross_out, cross_out_other]
    for step in range(groups - 1):
        cross_out += [turned[step], swap(handed[step])]
    pieces = call(
        lambda *refs: mlp_kernel(groups, images if static else 0, *refs),
        [shape((column, rows), F32)] * 2 + [shape((column, rows), BF16)] * (2 * groups - 2),
        [listed, *contexts, *cross_out, after, gain_mlp, w_up, up_other, w_down, down_other],
        scratch=[pltpu.VMEM((model, rows), F32)] * 2,
        smem=1,
        flops=3 * 10**9,
    )
    arrived = [pieces[0], swap(pieces[1])]
    for step in range(1, groups):
        arrived += [turn(pieces[2 * step], step), turn(pieces[2 * step + 1], step, 1)]
    summed = call(lambda *refs: sum_kernel(groups, *refs), shape((column, tokens), F32), arrived)
    return summed.T[None]


def solution(mesh):
    in_specs = (
        P(("grp", "pair"), None, "head"),
        P("grp", None),
        P(),
        P(),
        P(),
        P(),
        P(None, None, "head"),
        P("head", None),
        P(None, None, "head"),
        P("head", None),
        P(None, "head"),
        P("head", None),
    )
    out_specs = P(("grp", "pair"), None, "head")
    return jax.shard_map(body, mesh=mesh, in_specs=in_specs, out_specs=out_specs, check_vma=False)
```

```python
import math

import jax
import jax.numpy as jnp
from jax import lax
from jax.experimental import pallas as pl
from jax.experimental.pallas import tpu as pltpu
from jax.sharding import PartitionSpec as P

HEAD_DIM = 64
ROW_GROUPS = 2
DEGREE = 6
SCALE = 1.0 / math.sqrt(HEAD_DIM)
VMEM = pl.BlockSpec(memory_space=pltpu.VMEM)
SMEM = pl.BlockSpec(memory_space=pltpu.SMEM)
BF16 = jnp.bfloat16
F32 = jnp.float32


def mm(a, b):
    return jnp.dot(a, b, preferred_element_type=F32)


def standardize(x):
    centred = x - jnp.mean(x, axis=-1, keepdims=True)
    variance = jnp.mean(centred * centred, axis=-1, keepdims=True)
    return centred * lax.rsqrt(variance + 1e-06)


def head_attention(q, k, v):
    rows, width = q.shape
    heads = width // HEAD_DIM
    lane_head = lax.broadcasted_iota(jnp.int32, (rows, width), 1) // HEAD_DIM
    zero = jnp.zeros_like(q)
    stacked = jnp.concatenate([jnp.where(lane_head == i, q, zero) for i in range(heads)], axis=0)
    scores = lax.dot_general(stacked, k, (((1,), (1,)), ((), ())), preferred_element_type=F32)
    top = jnp.max(scores, axis=-1, keepdims=True)
    weights = jnp.exp((scores - top) * SCALE)
    total = jnp.sum(weights, axis=-1, keepdims=True)
    weights = (weights * (1.0 / total)).astype(BF16)
    mixed = mm(weights, v)
    context = jnp.zeros((rows, width), F32)
    for i in range(heads):
        context = context + jnp.where(lane_head == i, mixed[i * rows : (i + 1) * rows], 0.0)
    return context


def position():
    here = lax.axis_index("head")
    return here // ROW_GROUPS, lax.rem(here, ROW_GROUPS)


def mark_kernel(block, out):
    out[...] = block[:8, :128].astype(F32)


def memory_kernel(groups, *refs):
    blocks = refs[: 2 * groups]
    g_self, g_memory, w_qkv = refs[2 * groups : 2 * groups + 3]
    x_rows, normed_self, kv, x_full = refs[-4:]
    group, member = position()
    width = blocks[0].shape[0]
    for index in range(2 * groups):
        source = lax.rem(group - index // 2 + groups, groups) * 2
        source = source + (member if index % 2 == 0 else 1 - member)
        x_full[pl.ds(pl.multiple_of(source * width, width), width), :] = blocks[index][...]
    x = x_full[...].astype(F32).T
    rows = x.shape[0] // ROW_GROUPS
    x_rows[...] = jnp.where(member == 0, x[:rows], x[rows:])
    normed = standardize(x)
    memory = (normed * g_memory[...].reshape(1, -1)).astype(BF16)
    kv[:, : kv.shape[1] // 2] = mm(memory, w_qkv[1]).astype(BF16)
    kv[:, kv.shape[1] // 2 :] = mm(memory, w_qkv[2]).astype(BF16)
    normed_self[...] = (normed * g_self[...].reshape(1, -1)).astype(BF16)


def self_kernel(normed, w_own, w_other, out_own, out_other, partial):
    member = position()[1]
    own = normed[...]
    rows = own.shape[0] // ROW_GROUPS
    mine = jnp.where(member == 0, own[:rows], own[rows:])
    q = jnp.concatenate([mm(mine, w_own[0]), mm(mine, w_other[0])], axis=1).astype(BF16)
    k = jnp.concatenate([mm(own, w_own[1]), mm(own, w_other[1])], axis=1).astype(BF16)
    v = jnp.concatenate([mm(own, w_own[2]), mm(own, w_other[2])], axis=1).astype(BF16)
    context = head_attention(q, k, v).astype(BF16)
    width = context.shape[1] // 2
    total = mm(context[:, :width], out_own[...]) + mm(context[:, width:], out_other[...])
    partial[...] = total.astype(BF16)


def hand_on(passed, handed, sems):
    copies = [pltpu.make_async_copy(passed[i], handed[i], sems.at[i]) for i in range(len(passed))]
    for copy in copies:
        copy.start()
    return copies


def cross_kernel(groups, views, count, x_rows, gain, w_own, w_other, *refs):
    partials, refs = refs[:groups], refs[groups:]
    kv_own, kv_other, refs = refs[:views], refs[views : 2 * views], refs[2 * views :]
    passed, refs = refs[:count], refs[count:]
    after, context, handed, sems = refs[0], refs[1], refs[2:-1], refs[-1]
    if len(handed) < count:
        handed = [handed[0].at[0], handed[0].at[1], *handed[1:]]
    copies = hand_on(passed, handed, sems)
    total = x_rows[...]
    for partial in partials:
        total = total + partial[...].astype(F32)
    after[...] = total
    normed = (standardize(total) * gain[...].reshape(1, -1)).astype(BF16)
    q = jnp.concatenate([mm(normed, w_own[0]), mm(normed, w_other[0])], axis=1).astype(BF16)
    width = q.shape[1] // 2
    for view in range(views):
        k = jnp.concatenate([kv_own[view][:, :width], kv_other[view][:, :width]], axis=1)
        v = jnp.concatenate([kv_own[view][:, width:], kv_other[view][:, width:]], axis=1)
        context[view] = head_attention(q, k, v).astype(BF16)
    for copy in copies:
        copy.wait()


def other_image(image, step, images):
    return image ^ step if images & (images - 1) == 0 else (image + step) % images


def pair_steps(images):
    return [*range(2, images), 1]


def view_counts(images, pairs):
    image = lax.axis_index("pair")
    counts = []
    for step in pair_steps(images):
        memory = other_image(image, step, images)
        count = jnp.int32(0)
        for pair in range(pairs.shape[1]):
            first, second = pairs[0, pair], pairs[1, pair]
            named = ((first == image) & (second == memory)) | ((first == memory) & (second == image))
            count = count + jnp.where(named, 1, 0)
        counts.append(count.astype(F32))
    return counts


def mlp_kernel(groups, images, listed, *refs):
    contexts, refs = refs[:groups], refs[groups:]
    views, _, width = contexts[0].shape
    width = width // 2
    w_out = refs[: 2 * groups]
    after, gain, up_own, down_own = refs[2 * groups : 2 * groups + 4]
    others = refs[2 * groups + 4 : -2 * groups - 2]
    up_other, down_other = others if len(others) == 2 else (others[0].at[0], others[0].at[1])
    outs, (kept, partial) = refs[-2 * groups - 2 : -2], refs[-2:]
    group, member = position()
    rows = after.shape[0]
    column = after.shape[1] // (2 * groups)
    residual = after[...]
    total = jnp.concatenate([residual] * views, axis=0)
    for step in range(groups):
        held = contexts[step][...].reshape(views * rows, 2 * width)
        total = total + mm(held[:, :width], w_out[2 * step][...])
        total = total + mm(held[:, width:], w_out[2 * step + 1][...])
    if images:
        share = view_counts(images, listed)
    else:
        share = [listed[view].astype(F32) for view in range(views)]
    keep = jnp.zeros_like(residual)
    for view in range(views):
        keep = keep + share[view] * total[view * rows : (view + 1) * rows]
    kept[...] = keep.T
    normed = (standardize(total) * gain[...].reshape(1, -1)).astype(BF16)
    down = jnp.zeros_like(residual)
    for w_up, w_down in ((up_own, down_own), (up_other, down_other)):
        raw = mm(normed, w_up[...])
        hidden = (0.5 * raw * (1.0 + lax.erf(raw * math.sqrt(0.5)))).astype(BF16).astype(F32)
        added = jnp.zeros((rows, raw.shape[1]), F32)
        for view in range(views):
            added = added + share[view] * hidden[view * rows : (view + 1) * rows]
        down = down + mm(added.astype(BF16), w_down[...])
    partial[...] = down.T
    for step in range(groups):
        target = lax.rem(group + step, groups)
        for other in range(2):
            index = target * 2 + (member if other == 0 else 1 - member)
            here = pl.ds(pl.multiple_of(index * column, column), column)
            piece = partial[here, :]
            if step == 0:
                piece = piece + kept[here, :]
            outs[2 * step + other][...] = piece.astype(outs[2 * step + other].dtype)


def sum_kernel(groups, *refs):
    member = position()[1]
    out = refs[2 * groups]
    rows = refs[0].shape[1]
    mine, theirs = refs[0][...], refs[1][...]
    for step in range(1, groups):
        mine = mine + refs[2 * step][...].astype(F32)
        theirs = theirs + refs[2 * step + 1][...].astype(F32)
    out[:, :rows] = jnp.where(member == 0, mine, theirs)
    out[:, rows:] = jnp.where(member == 0, theirs, mine)


def body(
    features,
    pair_list,
    gain_self,
    gain_memory,
    gain_cross,
    gain_mlp,
    w_self_qkv,
    w_self_out,
    w_cross_qkv,
    w_cross_out,
    w_up,
    w_down,
):
    head = lax.axis_size("head")
    groups = head // ROW_GROUPS
    images = lax.axis_size("pair")
    tokens, column = features.shape[1:]
    model = gain_self.shape[0]
    rows = tokens // ROW_GROUPS
    att = w_self_out.shape[0]

    def swap(value):
        return lax.ppermute(value, "head", [(i, i ^ 1) for i in range(head)])

    def turn(value, step, cross=0):
        return lax.ppermute(
            value,
            "head",
            [
                (i, ((i // 2 + step) % groups) * 2 + ((i % 2) ^ cross))
                for i in range(head)
            ],
        )

    def call(kernel, out_shape, args, scratch=(), smem=0, flops=0, moved=0):
        return pl.pallas_call(
            kernel,
            out_shape=out_shape,
            in_specs=[SMEM] * smem + [VMEM] * (len(args) - smem),
            out_specs=jax.tree.map(lambda _: VMEM, out_shape),
            scratch_shapes=list(scratch),
            compiler_params=pltpu.CompilerParams(vmem_limit_bytes=16 * 2**20),
            cost_estimate=pl.CostEstimate(flops=flops, bytes_accessed=moved, transcendentals=0),
        )(*args)

    shape = jax.ShapeDtypeStruct
    features = features[0].T
    blocks = [features, swap(features)]
    for step in range(1, groups):
        arrived = turn(features, step)
        blocks += [arrived, swap(arrived)]
    turned = [turn(w_cross_out, step) for step in range(1, groups)]
    self_other, self_out_other, cross_other = swap(w_self_qkv), swap(w_self_out), swap(w_cross_qkv)
    cross_out_other = swap(w_cross_out)

    mark = call(mark_kernel, shape((8, 128), F32), [blocks[1]], flops=3 * 10**9)
    x_rows, normed_self, kv = call(
        lambda *refs: memory_kernel(groups, *refs),
        [shape((rows, model), F32), shape((tokens, model), BF16), shape((tokens, 2 * att), BF16)],
        [*blocks, gain_self, gain_memory, w_cross_qkv, mark, cross_other, cross_out_other],
        scratch=[pltpu.VMEM((model, tokens), BF16)],
        flops=10**8,
    )
    partial = call(
        self_kernel,
        shape((rows, model), BF16),
        [normed_self, w_self_qkv, self_other, w_self_out, self_out_other],
        flops=10**8,
    )

    static = images - 1 <= DEGREE
    if static:
        views = images - 1
        listed = pair_list.T
        kv_own = [
            lax.ppermute(kv, "pair", [(other_image(i, step, images), i) for i in range(images)])
            for step in pair_steps(images)
        ]
    else:
        views = min(DEGREE, pair_list.shape[0])
        image = lax.axis_index("pair")
        first, second = pair_list[:, 0], pair_list[:, 1]
        named = (first == image) | (second == image)
        partner = jnp.where(first == image, second, first)
        rank = jnp.cumsum(named.astype(jnp.int32)) - 1
        hit = named[None, :] & (rank[None, :] == jnp.arange(views)[:, None])
        memories = jnp.sum(jnp.where(hit, partner[None, :], 0), axis=1)
        listed = jnp.any(hit, axis=1).astype(jnp.int32)
        gathered = lax.all_gather(kv, "pair", axis=0, tiled=False)
        kv_own = [lax.dynamic_index_in_dim(gathered, memories[view], 0, False) for view in range(views)]
    partials = [partial] + [turn(partial, step) for step in range(1, groups)]
    late = [w_up, w_down, *turned]
    packed = w_up.shape == w_down.shape
    late_shapes = [shape(value.shape, BF16) for value in late]
    if packed:
        late_shapes = [shape((2, *w_up.shape), BF16), *late_shapes[2:]]
    after, context, *handed = call(
        lambda *refs: cross_kernel(groups, views, len(late), *refs),
        [shape((rows, model), F32), shape((views, rows, 2 * att), BF16)] + late_shapes,
        [
            x_rows,
            gain_cross,
            w_cross_qkv,
            cross_other,
            *partials,
            *kv_own,
            *[swap(value) for value in kv_own],
            *late,
        ],
        scratch=[pltpu.SemaphoreType.DMA((len(late),))],
        flops=10**8,
    )
    handed = [swap(value) for value in handed]
    mlp_other = handed[: 1 if packed else 2]
    cross_out = [w_cross_out, cross_out_other]
    for step in range(groups - 1):
        cross_out += [turned[step], handed[len(mlp_other) + step]]
    contexts = [context] + [turn(context, step) for step in range(1, groups)]
    pieces = call(
        lambda *refs: mlp_kernel(groups, images if static else 0, *refs),
        [shape((column, rows), F32)] * 2 + [shape((column, rows), BF16)] * (2 * groups - 2),
        [listed, *contexts, *cross_out, after, gain_mlp, w_up, w_down, *mlp_other],
        scratch=[pltpu.VMEM((model, rows), F32)] * 2,
        smem=1,
        flops=3 * 10**9,
    )
    arrived = [pieces[0], swap(pieces[1])]
    for step in range(1, groups):
        arrived += [turn(pieces[2 * step], step), turn(pieces[2 * step + 1], step, 1)]
    summed = call(lambda *refs: sum_kernel(groups, *refs), shape((column, tokens), F32), arrived)
    return summed.T[None]


def solution(mesh):
    in_specs = (
        P(("grp", "pair"), None, "head"),
        P("grp", None),
        P(),
        P(),
        P(),
        P(),
        P(None, None, "head"),
        P("head", None),
        P(None, None, "head"),
        P("head", None),
        P(None, "head"),
        P("head", None),
    )
    out_specs = P(("grp", "pair"), None, "head")
    return jax.shard_map(body, mesh=mesh, in_specs=in_specs, out_specs=out_specs, check_vma=False)
```

```python
import math

import jax
import jax.numpy as jnp
from jax import lax
from jax.experimental import pallas as pl
from jax.experimental.pallas import tpu as pltpu
from jax.sharding import PartitionSpec as P

HEAD_DIM = 64
ROW_GROUPS = 2
DEGREE = 6
SCALE = 1.0 / math.sqrt(HEAD_DIM)
VMEM = pl.BlockSpec(memory_space=pltpu.VMEM)
ANY = pl.BlockSpec(memory_space=pl.ANY)
SMEM = pl.BlockSpec(memory_space=pltpu.SMEM)
BF16 = jnp.bfloat16
F32 = jnp.float32


def mm(a, b):
    return jnp.dot(a, b, preferred_element_type=F32)


def standardize(x):
    centred = x - jnp.mean(x, axis=-1, keepdims=True)
    variance = jnp.mean(centred * centred, axis=-1, keepdims=True)
    return centred * lax.rsqrt(variance + 1e-06)


def head_attention(q, k, v):
    rows, width = q.shape
    heads = width // HEAD_DIM
    lane_head = lax.broadcasted_iota(jnp.int32, (rows, width), 1) // HEAD_DIM
    zero = jnp.zeros_like(q)
    stacked = jnp.concatenate([jnp.where(lane_head == i, q, zero) for i in range(heads)], axis=0)
    scores = lax.dot_general(stacked, k, (((1,), (1,)), ((), ())), preferred_element_type=F32)
    top = jnp.max(scores, axis=-1, keepdims=True)
    weights = jnp.exp((scores - top) * SCALE)
    total = jnp.sum(weights, axis=-1, keepdims=True)
    weights = (weights * (1.0 / total)).astype(BF16)
    mixed = mm(weights, v)
    context = jnp.zeros((rows, width), F32)
    for i in range(heads):
        context = context + jnp.where(lane_head == i, mixed[i * rows : (i + 1) * rows], 0.0)
    return context


def position():
    here = lax.axis_index("head")
    return here // ROW_GROUPS, lax.rem(here, ROW_GROUPS)


def mark_kernel(block, out):
    out[...] = block[:8, :128].astype(out.dtype)


def memory_kernel(groups, *refs):
    blocks = refs[: 2 * groups]
    g_self, g_memory, w_qkv = refs[2 * groups : 2 * groups + 3]
    x_rows, normed_self, kv, x_full = refs[-4:]
    group, member = position()
    width = blocks[0].shape[0]
    for index in range(2 * groups):
        source = lax.rem(group - index // 2 + groups, groups) * 2
        source = source + (member if index % 2 == 0 else 1 - member)
        x_full[pl.ds(pl.multiple_of(source * width, width), width), :] = blocks[index][...]
    x = x_full[...].astype(F32).T
    rows = x.shape[0] // ROW_GROUPS
    x_rows[...] = jnp.where(member == 0, x[:rows], x[rows:])
    normed = standardize(x)
    memory = (normed * g_memory[...].reshape(1, -1)).astype(BF16)
    kv[:, : kv.shape[1] // 2] = mm(memory, w_qkv[1]).astype(BF16)
    kv[:, kv.shape[1] // 2 :] = mm(memory, w_qkv[2]).astype(BF16)
    normed_self[...] = (normed * g_self[...].reshape(1, -1)).astype(BF16)


def self_kernel(normed, w_own, w_other, out_own, out_other, *refs):
    partial = refs[-1]
    member = position()[1]
    own = normed[...]
    rows = own.shape[0] // ROW_GROUPS
    mine = jnp.where(member == 0, own[:rows], own[rows:])
    q = jnp.concatenate([mm(mine, w_own[0]), mm(mine, w_other[0])], axis=1).astype(BF16)
    k = jnp.concatenate([mm(own, w_own[1]), mm(own, w_other[1])], axis=1).astype(BF16)
    v = jnp.concatenate([mm(own, w_own[2]), mm(own, w_other[2])], axis=1).astype(BF16)
    context = head_attention(q, k, v).astype(BF16)
    width = context.shape[1] // 2
    total = mm(context[:, :width], out_own[...]) + mm(context[:, width:], out_other[...])
    partial[...] = total.astype(BF16)


def query_kernel(groups, x_rows, gain, w_own, w_other, *refs):
    partials, packing, refs = refs[:groups], refs[groups : groups + 2], refs[groups + 2 :]
    after, queries, packed, sems = refs
    copies = [pltpu.make_async_copy(packing[i], packed.at[i], sems.at[i]) for i in range(2)]
    for copy in copies:
        copy.start()
    total = x_rows[...]
    for partial in partials:
        total = total + partial[...].astype(F32)
    after[...] = total
    normed = (standardize(total) * gain[...].reshape(1, -1)).astype(BF16)
    queries[...] = jnp.concatenate([mm(normed, w_own[0]), mm(normed, w_other[0])], axis=1).astype(BF16)
    for copy in copies:
        copy.wait()


def cross_kernel(first, views, total, queries, *refs):
    kv_own, kv_other, context = refs[first:], refs[total + first :], refs[-1]
    q = queries[...]
    width = q.shape[1] // 2
    for view in range(views):
        k = jnp.concatenate([kv_own[view][:, :width], kv_other[view][:, :width]], axis=1)
        v = jnp.concatenate([kv_own[view][:, width:], kv_other[view][:, width:]], axis=1)
        context[view] = head_attention(q, k, v).astype(BF16)


def other_image(image, step, images):
    return image ^ step if images & (images - 1) == 0 else (image + step) % images


def pair_steps(images):
    return [*range(2, images), 1]


def view_counts(images, pairs):
    image = lax.axis_index("pair")
    counts = []
    for step in pair_steps(images):
        memory = other_image(image, step, images)
        count = jnp.int32(0)
        for pair in range(pairs.shape[1]):
            first, second = pairs[0, pair], pairs[1, pair]
            named = ((first == image) & (second == memory)) | ((first == memory) & (second == image))
            count = count + jnp.where(named, 1, 0)
        counts.append(count.astype(F32))
    return counts


def mlp_kernel(groups, batches, shared, images, listed, *refs):
    count = groups * len(batches)
    contexts, w_out, refs = refs[:count], refs[count : count + 2 * groups], refs[count + 2 * groups :]
    after, gain, mlp_own, mlp_other = refs[:4]
    outs, (kept, partial) = refs[4:-2], refs[-2:]
    views, width = sum(batches), contexts[0].shape[2] // 2
    group, member = position()
    rows = after.shape[0]
    column = after.shape[1] // (2 * groups)
    residual = after[...]
    total = jnp.concatenate([residual] * views, axis=0)
    for step in range(groups):
        held = jnp.concatenate([block[...].reshape(-1, 2 * width) for block in contexts[step::groups]], axis=0)
        total = total + mm(held[:, :width], w_out[2 * step][...])
        total = total + mm(held[:, width:], w_out[2 * step + 1][...])
    if images:
        share = view_counts(images, listed)
    else:
        share = [listed[view].astype(F32) for view in range(views)]
    keep = jnp.zeros_like(residual)
    for view in range(views):
        keep = keep + share[view] * total[view * rows : (view + 1) * rows]
    kept[...] = keep.T
    normed = (standardize(total) * gain[...].reshape(1, -1)).astype(BF16)
    down = jnp.zeros_like(residual)
    for weights in (mlp_own, mlp_other):
        raw = mm(normed, weights[0])
        hidden = (0.5 * raw * (1.0 + lax.erf(raw * math.sqrt(0.5)))).astype(BF16).astype(F32)
        added = jnp.zeros((rows, raw.shape[1]), F32)
        for view in range(views):
            added = added + share[view] * hidden[view * rows : (view + 1) * rows]
        w_down = weights[1] if shared else weights[1].T
        down = down + mm(added.astype(BF16), w_down)
    partial[...] = down.T
    for step in range(groups):
        target = lax.rem(group + step, groups)
        for other in range(2):
            index = target * 2 + (member if other == 0 else 1 - member)
            here = pl.ds(pl.multiple_of(index * column, column), column)
            piece = partial[here, :]
            if step == 0:
                piece = piece + kept[here, :]
            outs[2 * step + other][...] = piece.astype(outs[2 * step + other].dtype)


def sum_kernel(groups, *refs):
    member = position()[1]
    out = refs[2 * groups]
    rows = refs[0].shape[1]
    mine, theirs = refs[0][...], refs[1][...]
    for step in range(1, groups):
        mine = mine + refs[2 * step][...].astype(F32)
        theirs = theirs + refs[2 * step + 1][...].astype(F32)
    out[:, :rows] = jnp.where(member == 0, mine, theirs)
    out[:, rows:] = jnp.where(member == 0, theirs, mine)


def body(
    features,
    pair_list,
    gain_self,
    gain_memory,
    gain_cross,
    gain_mlp,
    w_self_qkv,
    w_self_out,
    w_cross_qkv,
    w_cross_out,
    w_up,
    w_down,
):
    head = lax.axis_size("head")
    groups = head // ROW_GROUPS
    images = lax.axis_size("pair")
    tokens, column = features.shape[1:]
    model = gain_self.shape[0]
    rows = tokens // ROW_GROUPS
    att = w_self_out.shape[0]

    def swap(value):
        return lax.ppermute(value, "head", [(i, i ^ 1) for i in range(head)])

    def turn(value, step, cross=0):
        return lax.ppermute(
            value,
            "head",
            [
                (i, ((i // 2 + step) % groups) * 2 + ((i % 2) ^ cross))
                for i in range(head)
            ],
        )

    def call(kernel, out_shape, args, scratch=(), smem=0, flops=0, moved=0, aliases={}):
        return pl.pallas_call(
            kernel,
            out_shape=out_shape,
            in_specs=[SMEM] * smem + [VMEM] * (len(args) - smem - len(aliases)) + [ANY] * len(aliases),
            out_specs=[ANY if i in aliases.values() else VMEM for i in range(len(out_shape))],
            scratch_shapes=list(scratch),
            input_output_aliases=aliases,
            compiler_params=pltpu.CompilerParams(vmem_limit_bytes=16 * 2**20),
            cost_estimate=pl.CostEstimate(flops=flops, bytes_accessed=moved, transcendentals=0),
        )(*args)

    shape = jax.ShapeDtypeStruct
    features = features[0].T
    blocks = [features, swap(features)]
    for step in range(1, groups):
        arrived = turn(features, step)
        blocks += [arrived, swap(arrived)]
    turned = [turn(w_cross_out, step) for step in range(1, groups)]
    self_other, self_out_other, cross_other = swap(w_self_qkv), swap(w_self_out), swap(w_cross_qkv)
    cross_out_other = swap(w_cross_out)

    (mark,) = call(mark_kernel, [shape((8, 128), F32)], [blocks[1]], flops=3 * 10**9)
    (mark,) = call(mark_kernel, [shape((8, 128), F32)], [mark], flops=3 * 10**9)
    x_rows, normed_self, kv = call(
        lambda *refs: memory_kernel(groups, *refs),
        [shape((rows, model), F32), shape((tokens, model), BF16), shape((tokens, 2 * att), BF16)],
        [*blocks, gain_self, gain_memory, w_cross_qkv, mark, cross_other, cross_out_other],
        scratch=[pltpu.VMEM((model, tokens), BF16)],
        flops=10**8,
    )
    (partial,) = call(
        self_kernel,
        [shape((rows, model), BF16)],
        [normed_self, w_self_qkv, self_other, w_self_out, self_out_other, *turned],
        flops=10**8,
    )

    static = images - 1 <= DEGREE
    if static:
        views = images - 1
        listed = pair_list.T
        kv_own = [
            lax.ppermute(kv, "pair", [(other_image(i, step, images), i) for i in range(images)])
            for step in pair_steps(images)
        ]
    else:
        views = min(DEGREE, pair_list.shape[0])
        image = lax.axis_index("pair")
        first, second = pair_list[:, 0], pair_list[:, 1]
        named = (first == image) | (second == image)
        partner = jnp.where(first == image, second, first)
        rank = jnp.cumsum(named.astype(jnp.int32)) - 1
        hit = named[None, :] & (rank[None, :] == jnp.arange(views)[:, None])
        memories = jnp.sum(jnp.where(hit, partner[None, :], 0), axis=1)
        listed = jnp.any(hit, axis=1).astype(jnp.int32)
        gathered = lax.all_gather(kv, "pair", axis=0, tiled=False)
        kv_own = [lax.dynamic_index_in_dim(gathered, memories[view], 0, False) for view in range(views)]
    partials = [partial] + [turn(partial, step) for step in range(1, groups)]
    shared = w_up.shape == w_down.shape
    w_down_as_up = w_down if shared else w_down.T
    after, queries, packed = call(
        lambda *refs: query_kernel(groups, *refs),
        [shape((rows, model), F32), shape((rows, 2 * att), BF16), shape((2, *w_up.shape), BF16)],
        [x_rows, gain_cross, w_cross_qkv, cross_other, *partials, w_up, w_down_as_up],
        scratch=[pltpu.SemaphoreType.DMA((2,))],
        flops=10**8,
    )
    kv_other = [swap(value) for value in kv_own]
    passing = [packed, *turned]
    batches = [views - views // 3, views // 3] if views >= 3 else [views]
    contexts, done = [], 0
    for index, batch in enumerate(batches):
        args = [queries, *kv_own, *kv_other]
        out_shape = [shape((batch, rows, 2 * att), BF16)]
        aliases = {}
        if index == 0:
            aliases = {len(args) + i: i for i in range(len(passing))}
            args += passing
            out_shape = [shape(value.shape, BF16) for value in passing] + out_shape
        *passed, context = call(
            lambda *refs, done=done, batch=batch: cross_kernel(done, batch, views, *refs),
            out_shape,
            args,
            flops=10**8,
            aliases=aliases,
        )
        if index == 0:
            packed, turned = passed[0], passed[1:]
        contexts.append([context] + [turn(context, step) for step in range(1, groups)])
        done += batch
    packed_other = swap(packed)
    cross_out = [w_cross_out, cross_out_other]
    for value in turned:
        cross_out += [value, swap(value)]
    contexts = [context for batch in contexts for context in batch]
    pieces = call(
        lambda *refs: mlp_kernel(groups, batches, shared, images if static else 0, *refs),
        [shape((column, rows), F32)] * 2 + [shape((column, rows), BF16)] * (2 * groups - 2),
        [listed, *contexts, *cross_out, after, gain_mlp, packed, packed_other],
        scratch=[pltpu.VMEM((model, rows), F32)] * 2,
        smem=1,
        flops=3 * 10**9,
    )
    arrived = [pieces[0], swap(pieces[1])]
    for step in range(1, groups):
        arrived += [turn(pieces[2 * step], step), turn(pieces[2 * step + 1], step, 1)]
    (summed,) = call(lambda *refs: sum_kernel(groups, *refs), [shape((column, tokens), F32)], arrived)
    return summed.T[None]


def solution(mesh):
    in_specs = (
        P(("grp", "pair"), None, "head"),
        P("grp", None),
        P(),
        P(),
        P(),
        P(),
        P(None, None, "head"),
        P("head", None),
        P(None, None, "head"),
        P("head", None),
        P(None, "head"),
        P("head", None),
    )
    out_specs = P(("grp", "pair"), None, "head")
    return jax.shard_map(body, mesh=mesh, in_specs=in_specs, out_specs=out_specs, check_vma=False)
```

```python
import math

import jax
import jax.numpy as jnp
from jax import lax
from jax.experimental import pallas as pl
from jax.experimental.pallas import tpu as pltpu
from jax.sharding import PartitionSpec as P

HEAD_DIM = 64
ROW_GROUPS = 2
DEGREE = 6
SCALE = 1.0 / math.sqrt(HEAD_DIM)
VMEM = pl.BlockSpec(memory_space=pltpu.VMEM)
ANY = pl.BlockSpec(memory_space=pl.ANY)
SMEM = pl.BlockSpec(memory_space=pltpu.SMEM)
BF16 = jnp.bfloat16
F32 = jnp.float32


def mm(a, b):
    return jnp.dot(a, b, preferred_element_type=F32)


def standardize(x):
    centred = x - jnp.mean(x, axis=-1, keepdims=True)
    variance = jnp.mean(centred * centred, axis=-1, keepdims=True)
    return centred * lax.rsqrt(variance + 1e-06)


def head_attention(q, k, v):
    rows, width = q.shape
    heads = width // HEAD_DIM
    lane_head = lax.broadcasted_iota(jnp.int32, (rows, width), 1) // HEAD_DIM
    zero = jnp.zeros_like(q)
    stacked = jnp.concatenate([jnp.where(lane_head == i, q, zero) for i in range(heads)], axis=0)
    scores = lax.dot_general(stacked, k, (((1,), (1,)), ((), ())), preferred_element_type=F32)
    top = jnp.max(scores, axis=-1, keepdims=True)
    weights = jnp.exp((scores - top) * SCALE)
    total = jnp.sum(weights, axis=-1, keepdims=True)
    weights = (weights * (1.0 / total)).astype(BF16)
    mixed = mm(weights, v)
    context = jnp.zeros((rows, width), F32)
    for i in range(heads):
        context = context + jnp.where(lane_head == i, mixed[i * rows : (i + 1) * rows], 0.0)
    return context


def position():
    here = lax.axis_index("head")
    return here // ROW_GROUPS, lax.rem(here, ROW_GROUPS)


def mark_kernel(block, out):
    out[...] = block[:8, :128].astype(out.dtype)


def memory_kernel(groups, *refs):
    blocks = refs[: 2 * groups]
    g_self, g_memory, w_qkv = refs[2 * groups : 2 * groups + 3]
    x_rows, normed_self, kv, x_full = refs[-4:]
    group, member = position()
    width = blocks[0].shape[0]
    for index in range(2 * groups):
        source = lax.rem(group - index // 2 + groups, groups) * 2
        source = source + (member if index % 2 == 0 else 1 - member)
        x_full[pl.ds(pl.multiple_of(source * width, width), width), :] = blocks[index][...]
    x = x_full[...].astype(F32).T
    rows = x.shape[0] // ROW_GROUPS
    x_rows[...] = jnp.where(member == 0, x[:rows], x[rows:])
    normed = standardize(x)
    memory = (normed * g_memory[...].reshape(1, -1)).astype(BF16)
    kv[:, : kv.shape[1] // 2] = mm(memory, w_qkv[1]).astype(BF16)
    kv[:, kv.shape[1] // 2 :] = mm(memory, w_qkv[2]).astype(BF16)
    normed_self[...] = (normed * g_self[...].reshape(1, -1)).astype(BF16)


def self_kernel(groups, normed, w_own, w_other, out_own, out_other, *refs):
    packing, (partial, packed, sems) = refs[:groups], refs[groups:]
    copies = [pltpu.make_async_copy(packing[i], packed.at[i], sems.at[i]) for i in range(groups)]
    for copy in copies:
        copy.start()
    member = position()[1]
    own = normed[...]
    rows = own.shape[0] // ROW_GROUPS
    mine = jnp.where(member == 0, own[:rows], own[rows:])
    q = jnp.concatenate([mm(mine, w_own[0]), mm(mine, w_other[0])], axis=1).astype(BF16)
    k = jnp.concatenate([mm(own, w_own[1]), mm(own, w_other[1])], axis=1).astype(BF16)
    v = jnp.concatenate([mm(own, w_own[2]), mm(own, w_other[2])], axis=1).astype(BF16)
    context = head_attention(q, k, v).astype(BF16)
    width = context.shape[1] // 2
    total = mm(context[:, :width], out_own[...]) + mm(context[:, width:], out_other[...])
    partial[...] = total.astype(BF16)
    for copy in copies:
        copy.wait()


def query_kernel(groups, x_rows, gain, w_own, w_other, *refs):
    partials, packing, refs = refs[:groups], refs[groups : groups + 2], refs[groups + 2 :]
    after, queries, packed, sems = refs
    copies = [pltpu.make_async_copy(packing[i], packed.at[i], sems.at[i]) for i in range(2)]
    for copy in copies:
        copy.start()
    total = x_rows[...]
    for partial in partials:
        total = total + partial[...].astype(F32)
    after[...] = total
    normed = (standardize(total) * gain[...].reshape(1, -1)).astype(BF16)
    queries[...] = jnp.concatenate([mm(normed, w_own[0]), mm(normed, w_other[0])], axis=1).astype(BF16)
    for copy in copies:
        copy.wait()


def cross_kernel(first, views, total, queries, *refs):
    kv_own, kv_other, context = refs[first:], refs[total + first :], refs[-1]
    q = queries[...]
    width = q.shape[1] // 2
    for view in range(views):
        k = jnp.concatenate([kv_own[view][:, :width], kv_other[view][:, :width]], axis=1)
        v = jnp.concatenate([kv_own[view][:, width:], kv_other[view][:, width:]], axis=1)
        context[view] = head_attention(q, k, v).astype(BF16)


def other_image(image, step, images):
    return image ^ step if images & (images - 1) == 0 else (image + step) % images


def pair_steps(images):
    return [*range(2, images), 1]


def view_counts(images, pairs):
    image = lax.axis_index("pair")
    counts = []
    for step in pair_steps(images):
        memory = other_image(image, step, images)
        count = jnp.int32(0)
        for pair in range(pairs.shape[1]):
            first, second = pairs[0, pair], pairs[1, pair]
            named = ((first == image) & (second == memory)) | ((first == memory) & (second == image))
            count = count + jnp.where(named, 1, 0)
        counts.append(count.astype(F32))
    return counts


def mlp_kernel(groups, batches, shared, images, listed, *refs):
    count = groups * len(batches)
    contexts, refs = refs[:count], refs[count:]
    out_own, out_other, after, gain, mlp_own, mlp_other = refs[:6]
    outs, partial = refs[6:-1], refs[-1]
    views = sum(batches)
    group, member = position()
    rows = after.shape[0]
    column = after.shape[1] // (2 * groups)
    residual = after[...]
    held = jnp.concatenate(
        [
            jnp.concatenate([contexts[groups * batch + step][view] for step in range(groups)], axis=1)
            for batch in range(len(batches))
            for view in range(batches[batch])
        ],
        axis=0,
    )
    weight = jnp.concatenate([block[step] for step in range(groups) for block in (out_own, out_other)], axis=0)
    total = jnp.concatenate([residual] * views, axis=0) + mm(held, weight)
    if images:
        share = view_counts(images, listed)
    else:
        share = [listed[view].astype(F32) for view in range(views)]
    keep = jnp.zeros_like(residual)
    for view in range(views):
        keep = keep + share[view] * total[view * rows : (view + 1) * rows]
    normed = (standardize(total) * gain[...].reshape(1, -1)).astype(BF16)
    down = jnp.zeros_like(residual)
    for weights in (mlp_own, mlp_other):
        raw = mm(normed, weights[0])
        hidden = (0.5 * raw * (1.0 + lax.erf(raw * math.sqrt(0.5)))).astype(BF16).astype(F32)
        added = jnp.zeros((rows, raw.shape[1]), F32)
        for view in range(views):
            added = added + share[view] * hidden[view * rows : (view + 1) * rows]
        w_down = weights[1] if shared else weights[1].T
        down = down + mm(added.astype(BF16), w_down)
    source = lax.broadcasted_iota(jnp.int32, down.shape, 1) // (2 * column)
    partial[...] = jnp.where(source == group, down + keep, down).T
    for step in range(groups):
        target = lax.rem(group + step, groups)
        for other in range(2):
            index = target * 2 + (member if other == 0 else 1 - member)
            here = pl.ds(pl.multiple_of(index * column, column), column)
            outs[2 * step + other][...] = partial[here, :].astype(outs[2 * step + other].dtype)


def sum_kernel(groups, *refs):
    member = position()[1]
    out = refs[2 * groups]
    rows = refs[0].shape[1]
    mine, theirs = refs[0][...], refs[1][...]
    for step in range(1, groups):
        mine = mine + refs[2 * step][...].astype(F32)
        theirs = theirs + refs[2 * step + 1][...].astype(F32)
    out[:, :rows] = jnp.where(member == 0, mine, theirs)
    out[:, rows:] = jnp.where(member == 0, theirs, mine)


def body(
    features,
    pair_list,
    gain_self,
    gain_memory,
    gain_cross,
    gain_mlp,
    w_self_qkv,
    w_self_out,
    w_cross_qkv,
    w_cross_out,
    w_up,
    w_down,
):
    head = lax.axis_size("head")
    groups = head // ROW_GROUPS
    images = lax.axis_size("pair")
    tokens, column = features.shape[1:]
    model = gain_self.shape[0]
    rows = tokens // ROW_GROUPS
    att = w_self_out.shape[0]

    def swap(value):
        return lax.ppermute(value, "head", [(i, i ^ 1) for i in range(head)])

    def turn(value, step, cross=0):
        return lax.ppermute(
            value,
            "head",
            [
                (i, ((i // 2 + step) % groups) * 2 + ((i % 2) ^ cross))
                for i in range(head)
            ],
        )

    def call(kernel, out_shape, args, scratch=(), smem=0, flops=0, moved=0, aliases={}):
        return pl.pallas_call(
            kernel,
            out_shape=out_shape,
            in_specs=[SMEM] * smem + [VMEM] * (len(args) - smem - len(aliases)) + [ANY] * len(aliases),
            out_specs=[ANY if i in aliases.values() else VMEM for i in range(len(out_shape))],
            scratch_shapes=list(scratch),
            input_output_aliases=aliases,
            compiler_params=pltpu.CompilerParams(vmem_limit_bytes=16 * 2**20),
            cost_estimate=pl.CostEstimate(flops=flops, bytes_accessed=moved, transcendentals=0),
        )(*args)

    shape = jax.ShapeDtypeStruct
    features = features[0].T
    blocks = [features, swap(features)]
    for step in range(1, groups):
        arrived = turn(features, step)
        blocks += [arrived, swap(arrived)]
    turned = [turn(w_cross_out, step) for step in range(1, groups)]
    self_other, self_out_other, cross_other = swap(w_self_qkv), swap(w_self_out), swap(w_cross_qkv)

    (mark,) = call(mark_kernel, [shape((8, 128), F32)], [blocks[1]], flops=3 * 10**9)
    (mark,) = call(mark_kernel, [shape((8, 128), F32)], [mark], flops=3 * 10**9)
    x_rows, normed_self, kv = call(
        lambda *refs: memory_kernel(groups, *refs),
        [shape((rows, model), F32), shape((tokens, model), BF16), shape((tokens, 2 * att), BF16)],
        [*blocks, gain_self, gain_memory, w_cross_qkv, mark, cross_other],
        scratch=[pltpu.VMEM((model, tokens), BF16)],
        flops=10**8,
    )
    partial, out_own = call(
        lambda *refs: self_kernel(groups, *refs),
        [shape((rows, model), BF16), shape((groups, *w_cross_out.shape), BF16)],
        [normed_self, w_self_qkv, self_other, w_self_out, self_out_other, w_cross_out, *turned],
        scratch=[pltpu.SemaphoreType.DMA((groups,))],
        flops=10**8,
    )

    static = images - 1 <= DEGREE
    if static:
        views = images - 1
        listed = pair_list.T
        kv_own = [
            lax.ppermute(kv, "pair", [(other_image(i, step, images), i) for i in range(images)])
            for step in pair_steps(images)
        ]
    else:
        views = min(DEGREE, pair_list.shape[0])
        image = lax.axis_index("pair")
        first, second = pair_list[:, 0], pair_list[:, 1]
        named = (first == image) | (second == image)
        partner = jnp.where(first == image, second, first)
        rank = jnp.cumsum(named.astype(jnp.int32)) - 1
        hit = named[None, :] & (rank[None, :] == jnp.arange(views)[:, None])
        memories = jnp.sum(jnp.where(hit, partner[None, :], 0), axis=1)
        listed = jnp.any(hit, axis=1).astype(jnp.int32)
        gathered = lax.all_gather(kv, "pair", axis=0, tiled=False)
        kv_own = [lax.dynamic_index_in_dim(gathered, memories[view], 0, False) for view in range(views)]
    partials = [partial] + [turn(partial, step) for step in range(1, groups)]
    shared = w_up.shape == w_down.shape
    w_down_as_up = w_down if shared else w_down.T
    after, queries, mlp_own = call(
        lambda *refs: query_kernel(groups, *refs),
        [shape((rows, model), F32), shape((rows, 2 * att), BF16), shape((2, *w_up.shape), BF16)],
        [x_rows, gain_cross, w_cross_qkv, cross_other, *partials, w_up, w_down_as_up],
        scratch=[pltpu.SemaphoreType.DMA((2,))],
        flops=10**8,
    )
    kv_other = [swap(value) for value in kv_own]
    batches = [views - views // 3, views // 3] if views >= 3 else [views]
    contexts, done = [], 0
    for index, batch in enumerate(batches):
        args = [queries, *kv_own, *kv_other]
        out_shape = [shape((batch, rows, 2 * att), BF16)]
        aliases = {}
        if index == 0:
            passing = [mlp_own, out_own]
            aliases = {len(args) + i: i for i in range(2)}
            args += passing
            out_shape = [shape(value.shape, BF16) for value in passing] + out_shape
        *passed, context = call(
            lambda *refs, done=done, batch=batch: cross_kernel(done, batch, views, *refs),
            out_shape,
            args,
            flops=10**8,
            aliases=aliases,
        )
        if index == 0:
            mlp_own, out_own = passed
        contexts.append([context] + [turn(context, step) for step in range(1, groups)])
        done += batch
    contexts = [context for batch in contexts for context in batch]
    pieces = call(
        lambda *refs: mlp_kernel(groups, batches, shared, images if static else 0, *refs),
        [shape((column, rows), F32)] * 2 + [shape((column, rows), BF16)] * (2 * groups - 2),
        [listed, *contexts, out_own, swap(out_own), after, gain_mlp, mlp_own, swap(mlp_own)],
        scratch=[pltpu.VMEM((model, rows), F32)],
        smem=1,
        flops=3 * 10**9,
    )
    arrived = [pieces[0], swap(pieces[1])]
    for step in range(1, groups):
        arrived += [turn(pieces[2 * step], step), turn(pieces[2 * step + 1], step, 1)]
    (summed,) = call(lambda *refs: sum_kernel(groups, *refs), [shape((column, tokens), F32)], arrived)
    return summed.T[None]


def solution(mesh):
    in_specs = (
        P(("grp", "pair"), None, "head"),
        P("grp", None),
        P(),
        P(),
        P(),
        P(),
        P(None, None, "head"),
        P("head", None),
        P(None, None, "head"),
        P("head", None),
        P(None, "head"),
        P("head", None),
    )
    out_specs = P(("grp", "pair"), None, "head")
    return jax.shard_map(body, mesh=mesh, in_specs=in_specs, out_specs=out_specs, check_vma=False)
```

```python
import math

import jax
import jax.numpy as jnp
from jax import lax
from jax.experimental import pallas as pl
from jax.experimental.pallas import tpu as pltpu
from jax.sharding import PartitionSpec as P

HEAD_DIM = 64
ROW_GROUPS = 2
DEGREE = 6
SCALE = 1.0 / math.sqrt(HEAD_DIM)
VMEM = pl.BlockSpec(memory_space=pltpu.VMEM)
ANY = pl.BlockSpec(memory_space=pl.ANY)
SMEM = pl.BlockSpec(memory_space=pltpu.SMEM)
BF16 = jnp.bfloat16
F32 = jnp.float32


def mm(a, b):
    return jnp.dot(a, b, preferred_element_type=F32)


def standardize(x):
    centred = x - jnp.mean(x, axis=-1, keepdims=True)
    variance = jnp.mean(centred * centred, axis=-1, keepdims=True)
    return centred * lax.rsqrt(variance + 1e-06)


def head_attention(q, k, v):
    rows, width = q.shape
    heads = width // HEAD_DIM
    lane_head = lax.broadcasted_iota(jnp.int32, (rows, width), 1) // HEAD_DIM
    zero = jnp.zeros_like(q)
    stacked = jnp.concatenate([jnp.where(lane_head == i, q, zero) for i in range(heads)], axis=0)
    scores = lax.dot_general(stacked, k, (((1,), (1,)), ((), ())), preferred_element_type=F32)
    top = jnp.max(scores, axis=-1, keepdims=True)
    weights = jnp.exp((scores - top) * SCALE)
    total = jnp.sum(weights, axis=-1, keepdims=True)
    weights = (weights * (1.0 / total)).astype(BF16)
    mixed = mm(weights, v)
    context = jnp.zeros((rows, width), F32)
    for i in range(heads):
        context = context + jnp.where(lane_head == i, mixed[i * rows : (i + 1) * rows], 0.0)
    return context


def position():
    here = lax.axis_index("head")
    return here // ROW_GROUPS, lax.rem(here, ROW_GROUPS)


def mark_kernel(block, out):
    out[...] = block[:8, :128].astype(out.dtype)


def memory_kernel(groups, *refs):
    blocks = refs[: 2 * groups]
    g_self, g_memory, w_qkv = refs[2 * groups : 2 * groups + 3]
    x_rows, normed_self, kv, x_full = refs[-4:]
    group, member = position()
    width = blocks[0].shape[0]
    for index in range(2 * groups):
        source = lax.rem(group - index // 2 + groups, groups) * 2
        source = source + (member if index % 2 == 0 else 1 - member)
        x_full[pl.ds(pl.multiple_of(source * width, width), width), :] = blocks[index][...]
    x = x_full[...].astype(F32).T
    rows = x.shape[0] // ROW_GROUPS
    x_rows[...] = jnp.where(member == 0, x[:rows], x[rows:])
    normed = standardize(x)
    memory = (normed * g_memory[...].reshape(1, -1)).astype(BF16)
    kv[:, : kv.shape[1] // 2] = mm(memory, w_qkv[1]).astype(BF16)
    kv[:, kv.shape[1] // 2 :] = mm(memory, w_qkv[2]).astype(BF16)
    normed_self[...] = (normed * g_self[...].reshape(1, -1)).astype(BF16)


def self_kernel(groups, normed, w_own, w_other, out_own, out_other, *refs):
    packing, (partial, packed, sems) = refs[:groups], refs[groups:]
    copies = [pltpu.make_async_copy(packing[i], packed.at[i], sems.at[i]) for i in range(groups)]
    for copy in copies:
        copy.start()
    member = position()[1]
    own = normed[...]
    rows = own.shape[0] // ROW_GROUPS
    mine = jnp.where(member == 0, own[:rows], own[rows:])
    q = jnp.concatenate([mm(mine, w_own[0]), mm(mine, w_other[0])], axis=1).astype(BF16)
    k = jnp.concatenate([mm(own, w_own[1]), mm(own, w_other[1])], axis=1).astype(BF16)
    v = jnp.concatenate([mm(own, w_own[2]), mm(own, w_other[2])], axis=1).astype(BF16)
    context = head_attention(q, k, v).astype(BF16)
    width = context.shape[1] // 2
    total = mm(context[:, :width], out_own[...]) + mm(context[:, width:], out_other[...])
    partial[...] = total.astype(BF16)
    for copy in copies:
        copy.wait()


def query_kernel(groups, x_rows, gain, w_own, w_other, *refs):
    partials, packing, refs = refs[:groups], refs[groups : groups + 2], refs[groups + 2 :]
    after, queries, packed, sems = refs
    copies = [pltpu.make_async_copy(packing[i], packed.at[i], sems.at[i]) for i in range(2)]
    for copy in copies:
        copy.start()
    total = x_rows[...]
    for partial in partials:
        total = total + partial[...].astype(F32)
    after[...] = total
    normed = (standardize(total) * gain[...].reshape(1, -1)).astype(BF16)
    queries[...] = jnp.concatenate([mm(normed, w_own[0]), mm(normed, w_other[0])], axis=1).astype(BF16)
    for copy in copies:
        copy.wait()


def cross_kernel(first, views, total, queries, *refs):
    kv_own, kv_other, context = refs[first:], refs[total + first :], refs[-1]
    q = queries[...]
    width = q.shape[1] // 2
    for view in range(views):
        k = jnp.concatenate([kv_own[view][:, :width], kv_other[view][:, :width]], axis=1)
        v = jnp.concatenate([kv_own[view][:, width:], kv_other[view][:, width:]], axis=1)
        context[view] = head_attention(q, k, v).astype(BF16)


def other_image(image, step, images):
    return image ^ step if images & (images - 1) == 0 else (image + step) % images


def pair_steps(images):
    return [2, 1, *range(3, images)]


def view_counts(images, pairs):
    image = lax.axis_index("pair")
    counts = []
    for step in pair_steps(images):
        memory = other_image(image, step, images)
        count = jnp.int32(0)
        for pair in range(pairs.shape[1]):
            first, second = pairs[0, pair], pairs[1, pair]
            named = ((first == image) & (second == memory)) | ((first == memory) & (second == image))
            count = count + jnp.where(named, 1, 0)
        counts.append(count.astype(F32))
    return counts


def mlp_kernel(groups, batches, shared, images, listed, *refs):
    count = groups * len(batches)
    contexts, refs = refs[:count], refs[count:]
    out_own, out_other, after, gain, mlp_own, mlp_other = refs[:6]
    outs, partial = refs[6:-1], refs[-1]
    views = sum(batches)
    group, member = position()
    rows = after.shape[0]
    column = after.shape[1] // (2 * groups)
    residual = after[...]
    held = jnp.concatenate(
        [
            jnp.concatenate([contexts[groups * batch + step][view] for step in range(groups)], axis=1)
            for batch in range(len(batches))
            for view in range(batches[batch])
        ],
        axis=0,
    )
    weight = jnp.concatenate([block[step] for step in range(groups) for block in (out_own, out_other)], axis=0)
    total = jnp.concatenate([residual] * views, axis=0) + mm(held, weight)
    if images:
        share = view_counts(images, listed)
    else:
        share = [listed[view].astype(F32) for view in range(views)]
    keep = jnp.zeros_like(residual)
    for view in range(views):
        keep = keep + share[view] * total[view * rows : (view + 1) * rows]
    normed = (standardize(total) * gain[...].reshape(1, -1)).astype(BF16)
    down = jnp.zeros_like(residual)
    for weights in (mlp_own, mlp_other):
        raw = mm(normed, weights[0])
        hidden = (0.5 * raw * (1.0 + lax.erf(raw * math.sqrt(0.5)))).astype(BF16).astype(F32)
        added = jnp.zeros((rows, raw.shape[1]), F32)
        for view in range(views):
            added = added + share[view] * hidden[view * rows : (view + 1) * rows]
        w_down = weights[1] if shared else weights[1].T
        down = down + mm(added.astype(BF16), w_down)
    source = lax.broadcasted_iota(jnp.int32, down.shape, 1) // (2 * column)
    partial[...] = jnp.where(source == group, down + keep, down).T
    for step in range(groups):
        target = lax.rem(group + step, groups)
        for other in range(2):
            index = target * 2 + (member if other == 0 else 1 - member)
            here = pl.ds(pl.multiple_of(index * column, column), column)
            outs[2 * step + other][...] = partial[here, :].astype(outs[2 * step + other].dtype)


def sum_kernel(groups, *refs):
    member = position()[1]
    out = refs[2 * groups]
    rows = refs[0].shape[1]
    mine, theirs = refs[0][...], refs[1][...]
    for step in range(1, groups):
        mine = mine + refs[2 * step][...].astype(F32)
        theirs = theirs + refs[2 * step + 1][...].astype(F32)
    out[:, :rows] = jnp.where(member == 0, mine, theirs)
    out[:, rows:] = jnp.where(member == 0, theirs, mine)


def body(
    features,
    pair_list,
    gain_self,
    gain_memory,
    gain_cross,
    gain_mlp,
    w_self_qkv,
    w_self_out,
    w_cross_qkv,
    w_cross_out,
    w_up,
    w_down,
):
    head = lax.axis_size("head")
    groups = head // ROW_GROUPS
    images = lax.axis_size("pair")
    tokens, column = features.shape[1:]
    model = gain_self.shape[0]
    rows = tokens // ROW_GROUPS
    att = w_self_out.shape[0]

    def swap(value):
        return lax.ppermute(value, "head", [(i, i ^ 1) for i in range(head)])

    def turn(value, step, cross=0):
        return lax.ppermute(
            value,
            "head",
            [
                (i, ((i // 2 + step) % groups) * 2 + ((i % 2) ^ cross))
                for i in range(head)
            ],
        )

    def call(kernel, out_shape, args, scratch=(), smem=0, flops=0, moved=0, aliases={}):
        return pl.pallas_call(
            kernel,
            out_shape=out_shape,
            in_specs=[SMEM] * smem + [VMEM] * (len(args) - smem - len(aliases)) + [ANY] * len(aliases),
            out_specs=[ANY if i in aliases.values() else VMEM for i in range(len(out_shape))],
            scratch_shapes=list(scratch),
            input_output_aliases=aliases,
            compiler_params=pltpu.CompilerParams(vmem_limit_bytes=16 * 2**20),
            cost_estimate=pl.CostEstimate(flops=flops, bytes_accessed=moved, transcendentals=0),
        )(*args)

    shape = jax.ShapeDtypeStruct
    features = features[0].T
    blocks = [features, swap(features)]
    for step in range(1, groups):
        arrived = turn(features, step)
        blocks += [arrived, swap(arrived)]
    turned = [turn(w_cross_out, step) for step in range(1, groups)]
    self_other, self_out_other, cross_other = swap(w_self_qkv), swap(w_self_out), swap(w_cross_qkv)

    (mark,) = call(mark_kernel, [shape((8, 128), F32)], [blocks[1]], flops=3 * 10**9)
    (mark,) = call(mark_kernel, [shape((8, 128), F32)], [mark], flops=3 * 10**9)
    x_rows, normed_self, kv = call(
        lambda *refs: memory_kernel(groups, *refs),
        [shape((rows, model), F32), shape((tokens, model), BF16), shape((tokens, 2 * att), BF16)],
        [*blocks, gain_self, gain_memory, w_cross_qkv, mark, cross_other],
        scratch=[pltpu.VMEM((model, tokens), BF16)],
        flops=10**8,
    )
    partial, out_own = call(
        lambda *refs: self_kernel(groups, *refs),
        [shape((rows, model), BF16), shape((groups, *w_cross_out.shape), BF16)],
        [normed_self, w_self_qkv, self_other, w_self_out, self_out_other, w_cross_out, *turned],
        scratch=[pltpu.SemaphoreType.DMA((groups,))],
        flops=10**8,
    )

    static = images - 1 <= DEGREE
    if static:
        views = images - 1
        listed = pair_list.T
        kv_own = [
            lax.ppermute(kv, "pair", [(other_image(i, step, images), i) for i in range(images)])
            for step in pair_steps(images)
        ]
    else:
        views = min(DEGREE, pair_list.shape[0])
        image = lax.axis_index("pair")
        first, second = pair_list[:, 0], pair_list[:, 1]
        named = (first == image) | (second == image)
        partner = jnp.where(first == image, second, first)
        rank = jnp.cumsum(named.astype(jnp.int32)) - 1
        hit = named[None, :] & (rank[None, :] == jnp.arange(views)[:, None])
        memories = jnp.sum(jnp.where(hit, partner[None, :], 0), axis=1)
        listed = jnp.any(hit, axis=1).astype(jnp.int32)
        gathered = lax.all_gather(kv, "pair", axis=0, tiled=False)
        kv_own = [lax.dynamic_index_in_dim(gathered, memories[view], 0, False) for view in range(views)]
    partials = [partial] + [turn(partial, step) for step in range(1, groups)]
    shared = w_up.shape == w_down.shape
    w_down_as_up = w_down if shared else w_down.T
    after, queries, mlp_own = call(
        lambda *refs: query_kernel(groups, *refs),
        [shape((rows, model), F32), shape((rows, 2 * att), BF16), shape((2, *w_up.shape), BF16)],
        [x_rows, gain_cross, w_cross_qkv, cross_other, *partials, w_up, w_down_as_up],
        scratch=[pltpu.SemaphoreType.DMA((2,))],
        flops=10**8,
    )
    kv_other = [swap(value) for value in kv_own]
    batches = [views - views // 3, views // 3] if views >= 3 else [views]
    contexts, done = [], 0
    for index, batch in enumerate(batches):
        args = [queries, *kv_own, *kv_other]
        out_shape = [shape((batch, rows, 2 * att), BF16)]
        aliases = {}
        if index == 0:
            passing = [mlp_own, out_own]
            aliases = {len(args) + i: i for i in range(2)}
            args += passing
            out_shape = [shape(value.shape, BF16) for value in passing] + out_shape
        *passed, context = call(
            lambda *refs, done=done, batch=batch: cross_kernel(done, batch, views, *refs),
            out_shape,
            args,
            flops=10**8,
            aliases=aliases,
        )
        if index == 0:
            mlp_own, out_own = passed
        contexts.append([context] + [turn(context, step) for step in range(1, groups)])
        done += batch
    contexts = [context for batch in contexts for context in batch]
    pieces = call(
        lambda *refs: mlp_kernel(groups, batches, shared, images if static else 0, *refs),
        [shape((column, rows), F32)] * 2 + [shape((column, rows), BF16)] * (2 * groups - 2),
        [listed, *contexts, out_own, swap(out_own), after, gain_mlp, mlp_own, swap(mlp_own)],
        scratch=[pltpu.VMEM((model, rows), F32)],
        smem=1,
        flops=3 * 10**9,
    )
    arrived = [pieces[0], swap(pieces[1])]
    for step in range(1, groups):
        arrived += [turn(pieces[2 * step], step), turn(pieces[2 * step + 1], step, 1)]
    (summed,) = call(lambda *refs: sum_kernel(groups, *refs), [shape((column, tokens), F32)], arrived)
    return summed.T[None]


def solution(mesh):
    in_specs = (
        P(("grp", "pair"), None, "head"),
        P("grp", None),
        P(),
        P(),
        P(),
        P(),
        P(None, None, "head"),
        P("head", None),
        P(None, None, "head"),
        P("head", None),
        P(None, "head"),
        P("head", None),
    )
    out_specs = P(("grp", "pair"), None, "head")
    return jax.shard_map(body, mesh=mesh, in_specs=in_specs, out_specs=out_specs, check_vma=False)
```

```python
import math

import jax
import jax.numpy as jnp
from jax import lax
from jax.experimental import pallas as pl
from jax.experimental.pallas import tpu as pltpu
from jax.sharding import PartitionSpec as P

HEAD_DIM = 64
ROW_GROUPS = 2
DEGREE = 6
SCALE = 1.0 / math.sqrt(HEAD_DIM)
VMEM = pl.BlockSpec(memory_space=pltpu.VMEM)
ANY = pl.BlockSpec(memory_space=pl.ANY)
SMEM = pl.BlockSpec(memory_space=pltpu.SMEM)
BF16 = jnp.bfloat16
F32 = jnp.float32


def mm(a, b):
    return jnp.dot(a, b, preferred_element_type=F32)


def standardize(x):
    centred = x - jnp.mean(x, axis=-1, keepdims=True)
    variance = jnp.mean(centred * centred, axis=-1, keepdims=True)
    return centred * lax.rsqrt(variance + 1e-06)


def head_attention(q, k, v):
    rows, width = q.shape
    heads = width // HEAD_DIM
    lane_head = lax.broadcasted_iota(jnp.int32, (rows, width), 1) // HEAD_DIM
    zero = jnp.zeros_like(q)
    stacked = jnp.concatenate([jnp.where(lane_head == i, q, zero) for i in range(heads)], axis=0)
    scores = lax.dot_general(stacked, k, (((1,), (1,)), ((), ())), preferred_element_type=F32)
    top = jnp.max(scores, axis=-1, keepdims=True)
    weights = jnp.exp((scores - top) * SCALE)
    inverse = 1.0 / jnp.sum(weights, axis=-1, keepdims=True)
    mixed = mm(weights.astype(BF16), v)
    context = jnp.zeros((rows, width), F32)
    for i in range(heads):
        here = slice(i * rows, (i + 1) * rows)
        context = jnp.where(lane_head == i, mixed[here] * inverse[here], context)
    return context


def position():
    here = lax.axis_index("head")
    return here // ROW_GROUPS, lax.rem(here, ROW_GROUPS)


def mark_kernel(block, out):
    out[...] = block[:16, :128].astype(out.dtype)


def memory_kernel(groups, *refs):
    blocks = refs[: 2 * groups]
    g_self, g_memory, w_qkv = refs[2 * groups : 2 * groups + 3]
    x_rows, normed_self, kv, x_full = refs[-4:]
    group, member = position()
    width = blocks[0].shape[0]
    for index in range(2 * groups):
        source = lax.rem(group - index // 2 + groups, groups) * 2
        source = source + (member if index % 2 == 0 else 1 - member)
        x_full[pl.ds(pl.multiple_of(source * width, width), width), :] = blocks[index][...]
    x = x_full[...].astype(F32).T
    rows = x.shape[0] // ROW_GROUPS
    x_rows[...] = jnp.where(member == 0, x[:rows], x[rows:])
    normed = standardize(x)
    memory = (normed * g_memory[...].reshape(1, -1)).astype(BF16)
    kv[:, : kv.shape[1] // 2] = mm(memory, w_qkv[1]).astype(BF16)
    kv[:, kv.shape[1] // 2 :] = mm(memory, w_qkv[2]).astype(BF16)
    normed_self[...] = (normed * g_self[...].reshape(1, -1)).astype(BF16)


def self_kernel(groups, normed, w_own, w_other, out_own, out_other, *refs):
    packing, (partial, packed, sems) = refs[:groups], refs[groups:]
    copies = [pltpu.make_async_copy(packing[i], packed.at[i], sems.at[i]) for i in range(groups)]
    for copy in copies:
        copy.start()
    member = position()[1]
    own = normed[...]
    rows = own.shape[0] // ROW_GROUPS
    mine = jnp.where(member == 0, own[:rows], own[rows:])
    q = jnp.concatenate([mm(mine, w_own[0]), mm(mine, w_other[0])], axis=1).astype(BF16)
    k = jnp.concatenate([mm(own, w_own[1]), mm(own, w_other[1])], axis=1).astype(BF16)
    v = jnp.concatenate([mm(own, w_own[2]), mm(own, w_other[2])], axis=1).astype(BF16)
    context = head_attention(q, k, v).astype(BF16)
    width = context.shape[1] // 2
    total = mm(context[:, :width], out_own[...]) + mm(context[:, width:], out_other[...])
    partial[...] = total.astype(BF16)
    for copy in copies:
        copy.wait()


def query_kernel(groups, x_rows, gain, w_own, w_other, *refs):
    partials, packing, refs = refs[:groups], refs[groups : groups + 2], refs[groups + 2 :]
    after, queries, packed, sems = refs
    copies = [pltpu.make_async_copy(packing[i], packed.at[i], sems.at[i]) for i in range(2)]
    for copy in copies:
        copy.start()
    total = x_rows[...]
    for partial in partials:
        total = total + partial[...].astype(F32)
    after[...] = total
    normed = (standardize(total) * gain[...].reshape(1, -1)).astype(BF16)
    queries[...] = jnp.concatenate([mm(normed, w_own[0]), mm(normed, w_other[0])], axis=1).astype(BF16)
    for copy in copies:
        copy.wait()


def cross_kernel(first, views, total, queries, *refs):
    kv_own, kv_other, context = refs[first:], refs[total + first :], refs[-1]
    q = queries[...]
    width = q.shape[1] // 2
    for view in range(views):
        k = jnp.concatenate([kv_own[view][:, :width], kv_other[view][:, :width]], axis=1)
        v = jnp.concatenate([kv_own[view][:, width:], kv_other[view][:, width:]], axis=1)
        context[view] = head_attention(q, k, v).astype(BF16)


def other_image(image, step, images):
    return image ^ step if images & (images - 1) == 0 else (image + step) % images


def pair_steps(images):
    return sorted(range(1, images), key=lambda step: (step != 2, step))


def view_counts(images, pairs):
    image = lax.axis_index("pair")
    counts = []
    for step in pair_steps(images):
        memory = other_image(image, step, images)
        count = jnp.int32(0)
        for pair in range(pairs.shape[1]):
            first, second = pairs[0, pair], pairs[1, pair]
            named = ((first == image) & (second == memory)) | ((first == memory) & (second == image))
            count = count + jnp.where(named, 1, 0)
        counts.append(count.astype(F32))
    return counts


def mlp_kernel(groups, batches, shared, images, listed, *refs):
    count = groups * len(batches)
    contexts, refs = refs[:count], refs[count:]
    out_own, out_other, after, gain, mlp_own, mlp_other = refs[:6]
    outs, partial = refs[6:-1], refs[-1]
    views = sum(batches)
    group, member = position()
    rows = after.shape[0]
    column = after.shape[1] // (2 * groups)
    residual = after[...]
    att = out_own.shape[1]
    total = jnp.concatenate([residual] * views, axis=0)
    for other, weight in enumerate((out_own, out_other)):
        lanes = slice(other * att, (other + 1) * att)
        held = jnp.concatenate(
            [
                jnp.concatenate([contexts[groups * batch + step][view, :, lanes] for step in range(groups)], axis=1)
                for batch in range(len(batches))
                for view in range(batches[batch])
            ],
            axis=0,
        )
        total = total + mm(held, weight[...].reshape(groups * att, -1))
    if images:
        share = view_counts(images, listed)
    else:
        share = [listed[view].astype(F32) for view in range(views)]
    keep = jnp.zeros_like(residual)
    for view in range(views):
        keep = keep + share[view] * total[view * rows : (view + 1) * rows]
    normed = (standardize(total) * gain[...].reshape(1, -1)).astype(BF16)
    down = jnp.zeros_like(residual)
    for weights in (mlp_own, mlp_other):
        raw = mm(normed, weights[0])
        hidden = (0.5 * raw * (1.0 + lax.erf(raw * math.sqrt(0.5)))).astype(BF16).astype(F32)
        added = jnp.zeros((rows, raw.shape[1]), F32)
        for view in range(views):
            added = added + share[view] * hidden[view * rows : (view + 1) * rows]
        w_down = weights[1] if shared else weights[1].T
        down = down + mm(added.astype(BF16), w_down)
    source = lax.broadcasted_iota(jnp.int32, down.shape, 1) // (2 * column)
    partial[...] = jnp.where(source == group, down + keep, down).T
    for step in range(groups):
        target = lax.rem(group + step, groups)
        for other in range(2):
            index = target * 2 + (member if other == 0 else 1 - member)
            here = pl.ds(pl.multiple_of(index * column, column), column)
            outs[2 * step + other][...] = partial[here, :].astype(outs[2 * step + other].dtype)


def sum_kernel(groups, *refs):
    member = position()[1]
    out = refs[2 * groups]
    rows = refs[0].shape[1]
    mine, theirs = refs[0][...], refs[1][...]
    for step in range(1, groups):
        mine = mine + refs[2 * step][...].astype(F32)
        theirs = theirs + refs[2 * step + 1][...].astype(F32)
    out[:, :rows] = jnp.where(member == 0, mine, theirs)
    out[:, rows:] = jnp.where(member == 0, theirs, mine)


def body(
    features,
    pair_list,
    gain_self,
    gain_memory,
    gain_cross,
    gain_mlp,
    w_self_qkv,
    w_self_out,
    w_cross_qkv,
    w_cross_out,
    w_up,
    w_down,
):
    head = lax.axis_size("head")
    groups = head // ROW_GROUPS
    images = lax.axis_size("pair")
    tokens, column = features.shape[1:]
    model = gain_self.shape[0]
    rows = tokens // ROW_GROUPS
    att = w_self_out.shape[0]

    def swap(value):
        return lax.ppermute(value, "head", [(i, i ^ 1) for i in range(head)])

    def turn(value, step, cross=0):
        return lax.ppermute(
            value,
            "head",
            [
                (i, ((i // 2 + step) % groups) * 2 + ((i % 2) ^ cross))
                for i in range(head)
            ],
        )

    def call(kernel, out_shape, args, scratch=(), smem=0, flops=0, moved=0, aliases={}):
        return pl.pallas_call(
            kernel,
            out_shape=out_shape,
            in_specs=[SMEM] * smem + [VMEM] * (len(args) - smem - len(aliases)) + [ANY] * len(aliases),
            out_specs=[ANY if i in aliases.values() else VMEM for i in range(len(out_shape))],
            scratch_shapes=list(scratch),
            input_output_aliases=aliases,
            compiler_params=pltpu.CompilerParams(vmem_limit_bytes=16 * 2**20),
            cost_estimate=pl.CostEstimate(flops=flops, bytes_accessed=moved, transcendentals=0),
        )(*args)

    shape = jax.ShapeDtypeStruct
    features = features[0].T
    blocks = [features, swap(features)]
    for step in range(1, groups):
        arrived = turn(features, step)
        blocks += [arrived, swap(arrived)]
    turned = [turn(w_cross_out, step) for step in range(1, groups)]
    self_other, self_out_other, cross_other = swap(w_self_qkv), swap(w_self_out), swap(w_cross_qkv)

    (mark,) = call(mark_kernel, [shape((16, 128), F32)], [blocks[1]], flops=3 * 10**9)
    (mark,) = call(mark_kernel, [shape((16, 128), F32)], [mark], flops=3 * 10**9)
    x_rows, normed_self, kv = call(
        lambda *refs: memory_kernel(groups, *refs),
        [shape((rows, model), F32), shape((tokens, model), BF16), shape((tokens, 2 * att), BF16)],
        [*blocks, gain_self, gain_memory, w_cross_qkv, mark, cross_other],
        scratch=[pltpu.VMEM((model, tokens), BF16)],
        flops=10**8,
    )
    partial, out_own = call(
        lambda *refs: self_kernel(groups, *refs),
        [shape((rows, model), BF16), shape((groups, *w_cross_out.shape), BF16)],
        [normed_self, w_self_qkv, self_other, w_self_out, self_out_other, w_cross_out, *turned],
        scratch=[pltpu.SemaphoreType.DMA((groups,))],
        flops=10**8,
    )

    static = images - 1 <= DEGREE
    if static:
        views = images - 1
        listed = pair_list.T
        kv_own = [
            lax.ppermute(kv, "pair", [(other_image(i, step, images), i) for i in range(images)])
            for step in pair_steps(images)
        ]
    else:
        views = min(DEGREE, pair_list.shape[0])
        image = lax.axis_index("pair")
        first, second = pair_list[:, 0], pair_list[:, 1]
        named = (first == image) | (second == image)
        partner = jnp.where(first == image, second, first)
        rank = jnp.cumsum(named.astype(jnp.int32)) - 1
        hit = named[None, :] & (rank[None, :] == jnp.arange(views)[:, None])
        memories = jnp.sum(jnp.where(hit, partner[None, :], 0), axis=1)
        listed = jnp.any(hit, axis=1).astype(jnp.int32)
        gathered = lax.all_gather(kv, "pair", axis=0, tiled=False)
        kv_own = [lax.dynamic_index_in_dim(gathered, memories[view], 0, False) for view in range(views)]
    partials = [partial] + [turn(partial, step) for step in range(1, groups)]
    shared = w_up.shape == w_down.shape
    w_down_as_up = w_down if shared else w_down.T
    after, queries, mlp_own = call(
        lambda *refs: query_kernel(groups, *refs),
        [shape((rows, model), F32), shape((rows, 2 * att), BF16), shape((2, *w_up.shape), BF16)],
        [x_rows, gain_cross, w_cross_qkv, cross_other, *partials, w_up, w_down_as_up],
        scratch=[pltpu.SemaphoreType.DMA((2,))],
        flops=10**8,
    )
    kv_other = [swap(value) for value in kv_own]
    batches = [views - views // 3, views // 3] if views >= 3 else [views]
    contexts, done = [], 0
    for index, batch in enumerate(batches):
        args = [queries, *kv_own, *kv_other]
        out_shape = [shape((batch, rows, 2 * att), BF16)]
        aliases = {}
        if index == 0:
            passing = [mlp_own, out_own]
            aliases = {len(args) + i: i for i in range(2)}
            args += passing
            out_shape = [shape(value.shape, BF16) for value in passing] + out_shape
        *passed, context = call(
            lambda *refs, done=done, batch=batch: cross_kernel(done, batch, views, *refs),
            out_shape,
            args,
            flops=10**8,
            aliases=aliases,
        )
        if index == 0:
            mlp_own, out_own = passed
        contexts.append([context] + [turn(context, step) for step in range(1, groups)])
        done += batch
    contexts = [context for batch in contexts for context in batch]
    pieces = call(
        lambda *refs: mlp_kernel(groups, batches, shared, images if static else 0, *refs),
        [shape((column, rows), F32)] * 2 + [shape((column, rows), BF16)] * (2 * groups - 2),
        [listed, *contexts, out_own, swap(out_own), after, gain_mlp, mlp_own, swap(mlp_own)],
        scratch=[pltpu.VMEM((model, rows), F32)],
        smem=1,
        flops=3 * 10**9,
    )
    arrived = [pieces[0], swap(pieces[1])]
    for step in range(1, groups):
        arrived += [turn(pieces[2 * step], step), turn(pieces[2 * step + 1], step, 1)]
    (summed,) = call(lambda *refs: sum_kernel(groups, *refs), [shape((column, tokens), F32)], arrived)
    return summed.T[None]


def solution(mesh):
    in_specs = (
        P(("grp", "pair"), None, "head"),
        P("grp", None),
        P(),
        P(),
        P(),
        P(),
        P(None, None, "head"),
        P("head", None),
        P(None, None, "head"),
        P("head", None),
        P(None, "head"),
        P("head", None),
    )
    out_specs = P(("grp", "pair"), None, "head")
    return jax.shard_map(body, mesh=mesh, in_specs=in_specs, out_specs=out_specs, check_vma=False)
```
